128 devices in a mesh: rep: 16 (over y, z_hi, core), tp: 8 (over x, z_lo).
Axes of the slice: x: 4, y: 4, z: 4 (z_hi: 2, z_lo: 2; z = z_hi * 2 + z_lo), core: 2. Of those that a mesh axis runs over, the one named last changes fastest.
Arguments:
- inputs: bfloat16 [4, 1024, 5120], P(None, 'rep'), may hold values from -6 to 6
- qkv_weight: bfloat16 [2, 5120, 6144], P(None, ('rep', 'tp')), may hold values from -0.078125 to 0.078125
- out_weight: bfloat16 [2, 5120, 4096], P(None, ('rep', 'tp')), may hold values from -0.25 to 0.25
- norm_gain: float32 [2, 5120], replicated, may hold values from 0.1 to 1.9
- query_gain: float32 [2, 128], replicated, may hold values from 0.5 to 2
- key_gain: float32 [2, 128], replicated, may hold values from 0.5 to 2
- stored_rotated_keys: bfloat16 [2, 1024, 8, 256, 128], P(None, 'rep', 'tp'), may hold values from -540 to 540
- stored_cache_values: bfloat16 [2, 1024, 8, 256, 128], P(None, 'rep', 'tp'), may hold values from -6 to 6
- lengths: int32 [1024], P('rep'), may hold values from 1 to 256, as said below
Outputs:
- final_hidden: bfloat16 [4, 1024, 5120], P(None, 'rep')
The draws below stay inside these ranges and needn't reach their ends.
Inputs may be any that keep to these rules, and one draw needn't show every extreme that they name: `lengths`: in every replica some row has exactly 256 cached positions.
All inputs are finite; a program needn't handle non-finite values.
Results may differ from the reference program's by a relative error of at most 0.039.
The reference program's roundings to bfloat16 on the way count: a program that leaves them out, or rounds other values in their place, can miss the bound.
Values may be sent and summed in bfloat16 or wider, within the bound.
A program may use at most 192 MiB of HBM per device.

```python
import math
import jax
import jax.numpy as jnp
from jax import lax

D = 5120
KEY_VALUE_HEADS = 8
HEAD_SIZE = 128
HQ = 32
LAYER_COUNT = 2
STEPS = 4
REPLICA_ROWS = 64
CACHE_SLOTS = 256
REPLICA_ROW_TOTAL = 1024
QKV = 6144
N_REP = 16


def draw_stored_rotated_keys(key, part):
    key = jax.random.fold_in(key, 11)
    leading_shape, trailing_shape = jax.random.split(key)
    maximum_score = math.log(4.0)
    scale_factors = jnp.exp(jax.random.uniform(leading_shape, (LAYER_COUNT, REPLICA_ROW_TOTAL, KEY_VALUE_HEADS, 1, 1), jnp.float32, 0.0, maximum_score))
    value_rows = jax.random.truncated_normal(trailing_shape, -6.0, 6.0, (LAYER_COUNT, REPLICA_ROW_TOTAL, KEY_VALUE_HEADS, CACHE_SLOTS, HEAD_SIZE), jnp.float32)
    return (value_rows * scale_factors).astype(jnp.bfloat16)


def draw_lengths(key, part):
    key = jax.random.fold_in(key, 5)
    leading_shape, trailing_shape = jax.random.split(key)
    drawn = jax.random.randint(leading_shape, (REPLICA_ROW_TOTAL,), 1, CACHE_SLOTS + 1)
    offsets = jax.random.randint(trailing_shape, (REPLICA_ROW_TOTAL // REPLICA_ROWS, 1), 0, REPLICA_ROWS)
    filled = jnp.arange(REPLICA_ROWS, dtype=jnp.int32)[None, :] == offsets
    return jnp.where(filled.reshape(REPLICA_ROW_TOTAL), CACHE_SLOTS, drawn).astype(jnp.int32)


def levels(own_key, shape, shards, least, largest):
    factor_of, own = 1.0, jax.random.fold_in(own_key, 6)
    for dim, parts in shards:
        draws = jnp.exp(jax.random.uniform(jax.random.fold_in(own, dim), (parts,), jnp.float32, least / len(shards), largest / len(shards)))
        factor_of = factor_of * jnp.repeat(draws, shape[dim] // parts).reshape([-1 if axis == dim else 1 for axis in range(len(shape))])
    return factor_of


def gaussian(stream_key, extent, deviation, reach, pieces=(), held_as=jnp.bfloat16):
    loudness = levels(stream_key, extent, pieces, -0.22, 0.18) if pieces else 1.0
    values = jax.random.normal(stream_key, extent, jnp.float32) * deviation * loudness
    return jnp.minimum(jnp.maximum(values, -reach), reach).astype(held_as)


def setup_inputs(seed: int = 0) -> dict:
    seeds = jax.random.split(jax.random.key(seed), 10)
    return {
        "inputs": gaussian(seeds[0], (STEPS, REPLICA_ROW_TOTAL, D), 1.0, 6.0, ((1, 16),)),
        "qkv_weight": gaussian(seeds[1], (LAYER_COUNT, D, QKV), D ** -0.5, 0.078125, ((1, 128),)),
        "out_weight": gaussian(seeds[2], (LAYER_COUNT, D, HQ * HEAD_SIZE), (HQ * HEAD_SIZE // 8) ** -0.5, 0.25, ((1, 128),)),
        "norm_gain": jnp.clip(1.0 + 0.18 * jax.random.normal(seeds[3], (LAYER_COUNT, D), jnp.float32), 0.1, 1.9),
        "query_gain": jnp.clip(jnp.exp(jax.random.uniform(seeds[4], (LAYER_COUNT, HEAD_SIZE), jnp.float32, math.log(0.5), math.log(2.0))), 0.5, 2.0),
        "key_gain": jnp.clip(jnp.exp(jax.random.uniform(seeds[5], (LAYER_COUNT, HEAD_SIZE), jnp.float32, math.log(0.5), math.log(2.0))), 0.5, 2.0),
        "stored_rotated_keys": draw_stored_rotated_keys(jax.random.fold_in(seeds[9], 71), 0),
        "stored_cache_values": gaussian(seeds[7], (LAYER_COUNT, REPLICA_ROW_TOTAL, KEY_VALUE_HEADS, CACHE_SLOTS, HEAD_SIZE), 1.0, 6.0, ((1, 16), (2, 8))),
        "lengths": draw_lengths(jax.random.fold_in(seeds[9], 71), 0),
    }


epsilon = 1e-06
rope_base = 1000000.0

def rms_scale(value_rows, gain):
    wide = value_rows.astype(jnp.float32)
    return wide * lax.rsqrt(lax.optimization_barrier(jnp.mean(wide * wide, axis=-1, keepdims=True)) + epsilon) * gain

def rotate(value_rows, positions):
    half_dim = value_rows.shape[-1] // 2
    frequency = rope_base ** (-jnp.arange(half_dim, dtype=jnp.float32) / half_dim)
    angles = positions.astype(jnp.float32)[..., None] * frequency
    cosine = jnp.cos(angles)
    sine = jnp.sin(angles)
    leading_shape = value_rows[..., :half_dim]
    trailing_shape = value_rows[..., half_dim:]
    return jnp.concatenate([leading_shape * cosine - trailing_shape * sine, trailing_shape * cosine + leading_shape * sine], axis=-1)

def attend(queries, new_keys, new_values, old_keys, old_values, lengths):
    step_count = queries.shape[0]
    head_dim = queries.shape[-1]
    slots = old_keys.shape[2]
    queries_wide = queries.astype(jnp.float32)
    score_old = jnp.einsum('srkgd,rkcd->srkgc', queries_wide, old_keys.astype(jnp.float32)) * head_dim ** (-0.5)
    score_new = jnp.einsum('srkgd,trkd->srkgt', queries_wide, new_keys.astype(jnp.float32)) * head_dim ** (-0.5)
    live = jnp.arange(slots, dtype=jnp.int32)[None, :] < lengths[:, None]
    score_old = jnp.where(live[None, :, None, None, :], score_old, -jnp.inf)
    order = jnp.arange(step_count, dtype=jnp.int32)
    causal = order[None, :] <= order[:, None]
    score_new = jnp.where(causal[:, None, None, None, :], score_new, -jnp.inf)
    highest = jnp.maximum(lax.optimization_barrier(jnp.max(score_old, axis=-1)), lax.optimization_barrier(jnp.max(score_new, axis=-1)))[..., None]
    weight_old = jnp.exp(score_old - highest)
    weight_new = jnp.exp(score_new - highest)
    denominator = lax.optimization_barrier(jnp.sum(weight_old, axis=-1, keepdims=True)) + lax.optimization_barrier(jnp.sum(weight_new, axis=-1, keepdims=True))
    share_old = (weight_old / denominator).astype(jnp.bfloat16)
    share_new = (weight_new / denominator).astype(jnp.bfloat16)
    mixed = jnp.einsum('srkgc,rkcd->srkgd', share_old.astype(jnp.float32), old_values.astype(jnp.float32))
    mixed = mixed + jnp.einsum('srkgt,trkd->srkgd', share_new.astype(jnp.float32), new_values.astype(jnp.float32))
    return mixed.astype(jnp.bfloat16)

def decode_replica(hidden, old_keys, old_values, lengths, qkv_weight, out_weight, norm_gain, query_gain, key_gain):
    step_count = hidden.shape[0]
    row_count = hidden.shape[1]
    model_width = hidden.shape[2]
    groups = old_keys.shape[2]
    head_dim = old_keys.shape[4]
    per_group = qkv_weight.shape[2] // (groups * head_dim)
    positions = lengths[None, :] + jnp.arange(step_count, dtype=jnp.int32)[:, None]
    for layer_index in range(qkv_weight.shape[0]):
        normed = rms_scale(hidden, norm_gain[layer_index]).astype(jnp.bfloat16)
        mixed = jnp.dot(normed.reshape(step_count * row_count, model_width), qkv_weight[layer_index], preferred_element_type=jnp.float32)
        mixed = mixed.reshape(step_count, row_count, groups, per_group, head_dim)
        queries = rotate(rms_scale(mixed[:, :, :, :per_group - 2], query_gain[layer_index]), positions[:, :, None, None]).astype(jnp.bfloat16)
        new_keys = rotate(rms_scale(mixed[:, :, :, per_group - 2], key_gain[layer_index]), positions[:, :, None]).astype(jnp.bfloat16)
        new_values = mixed[:, :, :, per_group - 1].astype(jnp.bfloat16)
        attended = attend(queries, new_keys, new_values, old_keys[layer_index], old_values[layer_index], lengths)
        attended = attended.reshape(step_count * row_count, -1)
        projected = lax.dot_general(attended, out_weight[layer_index], (((1,), (1,)), ((), ())), preferred_element_type=jnp.float32)
        hidden = (hidden.astype(jnp.float32) + projected.reshape(step_count, row_count, model_width)).astype(jnp.bfloat16)
    return hidden

def reference(inputs, qkv_weight, out_weight, norm_gain, query_gain, key_gain, stored_rotated_keys, stored_cache_values, lengths):
    hidden_groups = inputs.reshape(STEPS, N_REP, REPLICA_ROWS, D).transpose(1, 0, 2, 3)
    grouped_keys = jnp.moveaxis(stored_rotated_keys.reshape(LAYER_COUNT, N_REP, REPLICA_ROWS, KEY_VALUE_HEADS, CACHE_SLOTS, HEAD_SIZE), 1, 0)
    grouped_values = jnp.moveaxis(stored_cache_values.reshape(LAYER_COUNT, N_REP, REPLICA_ROWS, KEY_VALUE_HEADS, CACHE_SLOTS, HEAD_SIZE), 1, 0)
    length_groups = lengths.reshape(N_REP, REPLICA_ROWS)

    def one_replica(group):
        return decode_replica(group[0], group[1], group[2], group[3], qkv_weight, out_weight, norm_gain, query_gain, key_gain)
    result = lax.map(one_replica, (hidden_groups, grouped_keys, grouped_values, length_groups))
    return result.transpose(1, 0, 2, 3).reshape(STEPS, REPLICA_ROW_TOTAL, D)
```

```python
import functools

import jax
import jax.numpy as jnp
from jax import lax
from jax.experimental import pallas as pl
from jax.experimental.pallas import tpu as pltpu
from jax.sharding import PartitionSpec as P

MESH = pl.DeviceIdType.MESH
epsilon = 1e-06
rope_base = 1000000.0

LAYERS = 2
STEPS = 4
ROWS = 64
FLAT = STEPS * ROWS
D = 5120
CHUNKS = 8
CHUNK = D // CHUNKS
OWN = 40
PAD = 48
HEAD = 128
GROUP = 768
ATT = 512
SLOTS = 256
HALF = 2048
TP = 8
f32 = jnp.float32
bf16 = jnp.bfloat16

NT = (((1,), (1,)), ((), ()))


def kernel(
    x_hbm, qw, ow, resid, gain, qgain, kgain, cosf, sinf, len16, k_hbm, v_hbm,
    out,
    wq, wo, land_q, land_o, pack, xin, norm, hid, hown, att, kbuf, vbuf, qs, ao, nk, nv, mixed,
    a2a_s, a2a_r, ex_s, ex_r, q_s, q_r, o_s, o_r, g_s, g_r, loc,
):
    r = lax.axis_index("rep")
    t = lax.axis_index("tp")
    y = lax.div(r, 4)
    zh = lax.rem(lax.div(r, 2), 2)
    c = lax.rem(r, 2)
    p = lax.div(r, 2)
    x = lax.div(t, 2)
    zl = lax.rem(t, 2)

    def rep(y_, zh_, c_):
        return y_ * 4 + zh_ * 2 + c_

    yp, ym, y2 = lax.rem(y + 1, 4), lax.rem(y + 3, 4), lax.rem(y + 2, 4)
    xp, xm = lax.rem(x + 1, 4), lax.rem(x + 3, 4)
    dev_yp = (rep(yp, zh, c), t)
    dev_ym = (rep(ym, zh, c), t)
    dev_z = (rep(y, 1 - zh, c), t)
    dev_sib = (rep(y, zh, 1 - c), t)
    dev_xp = (r, xp * 2 + zl)
    dev_xm = (r, xm * 2 + zl)
    dev_zl = (r, x * 2 + 1 - zl)

    sent = []

    def send(src, dst, ss, rs, dev):
        copy = pltpu.make_async_remote_copy(
            src_ref=src, dst_ref=dst, send_sem=ss, recv_sem=rs, device_id=dev, device_id_type=MESH
        )
        copy.start()
        sent.append(copy)

    def got(ref, rs):
        pltpu.make_async_remote_copy(
            src_ref=ref, dst_ref=ref, send_sem=rs, recv_sem=rs, device_id=dev_sib, device_id_type=MESH
        ).wait_recv()

    barrier = pltpu.get_barrier_semaphore()
    greet = [dev_yp, dev_ym, dev_z, dev_sib]
    for k in range(1, TP):
        other = lax.rem(t + k, TP)
        greet.append((r, other))
        greet.append((rep(y, zh, 1 - c), other))
    for dev in greet:
        pl.semaphore_signal(barrier, inc=1, device_id=dev, device_id_type=MESH)
    pl.semaphore_wait(barrier, len(greet))

    load_x = pltpu.make_async_copy(x_hbm, xin, loc.at[0])
    load_x.start()
    kv = {}

    def load_kv(layer):
        kv[layer] = [
            pltpu.make_async_copy(k_hbm.at[layer], kbuf, loc.at[1]),
            pltpu.make_async_copy(v_hbm.at[layer], vbuf, loc.at[2]),
        ]
        for copy in kv[layer]:
            copy.start()

    def qcols(other):
        return pl.ds(pl.multiple_of(other * GROUP, GROUP), GROUP)

    half_of_t = lax.div(t, 4)
    slot1 = lax.rem(t, 4) * 2 + c
    for k in range(1, TP):
        other = lax.rem(t + k, TP)
        send(qw.at[0, :, qcols(other)], land_q.at[0, t], a2a_s.at[0, k], a2a_r.at[0, t], (r, other))
    own0 = pltpu.make_async_copy(qw.at[0, :, qcols(t)], land_q.at[0, t], a2a_r.at[0, t])
    own0.start()
    load_kv(0)

    def start_exchange():
        for layer in range(LAYERS):
            theirs = pl.ds(pl.multiple_of((1 - c) * HALF, HALF), HALF)
            mine = pl.ds(pl.multiple_of(c * HALF, HALF), HALF)
            send(ow.at[layer, :, theirs], land_o.at[layer, c], ex_s.at[layer], ex_r.at[layer, c], dev_sib)
            pltpu.make_async_copy(ow.at[layer, :, mine], land_o.at[layer, c], ex_r.at[layer, 2]).start()

    def sibling_slab():
        return pltpu.make_async_remote_copy(
            src_ref=qw.at[1, :, qcols(t)], dst_ref=land_q.at[1, slot1], send_sem=a2a_s.at[1, 0],
            recv_sem=a2a_r.at[1, slot1], device_id=dev_sib, device_id_type=MESH,
        )

    def start_second():
        for k in range(1, TP):
            other = lax.rem(t + k, TP)
            send(
                qw.at[1, :, qcols(other)], land_q.at[1, slot1], a2a_s.at[1, k], a2a_r.at[1, slot1],
                (rep(y, zh, half_of_t), other),
            )

        @pl.when(half_of_t == c)
        def _():
            pltpu.make_async_copy(qw.at[1, :, qcols(t)], land_q.at[1, slot1], a2a_r.at[1, slot1]).start()

        @pl.when(half_of_t != c)
        def _():
            sibling_slab().start()

    def pack_q(layer):
        for slot in range(TP):
            got(land_q.at[layer, slot], a2a_r.at[layer, slot])
        for slot in range(TP):
            pack[slot * OWN : (slot + 1) * OWN, :] = land_q[layer, slot].astype(f32)[:OWN]
        if layer == 0:
            wq[0, p, pl.ds(pl.multiple_of(c * 320, 320), 320), :] = pack[...].astype(bf16)
        else:
            for k in range(4):
                wq[1, 4 * c + k, pl.ds(pl.multiple_of(p * 80, 80), 80), :] = pack[k * 80 : (k + 1) * 80, :].astype(bf16)

    def pack_o(layer):
        pltpu.make_async_copy(ow.at[layer, :, pl.ds(0, HALF)], land_o.at[layer, c], ex_r.at[layer, 2]).wait()
        got(land_o.at[layer, 1 - c], ex_r.at[layer, 1 - c])
        for cut in range(4):
            cols = slice(cut * 512, (cut + 1) * 512)
            both = jnp.concatenate(
                [land_o[layer, core, :, cols].astype(f32)[:OWN] for core in range(2)], axis=0
            )
            wo[layer, c, pl.ds(pl.multiple_of(p * 80, 80), 80), cols] = both.astype(bf16)

    def qblk(layer, y_, zh_, core):
        if layer == 0:
            return wq.at[0, y_ * 2 + zh_, pl.ds(pl.multiple_of(core * 320, 320), 320), :]
        return wq.at[1, pl.ds(4 * core, 4), pl.ds(pl.multiple_of((y_ * 2 + zh_) * 80, 80), 80), :]

    ring_y = [y, yp, y2, ym]

    def zsel(e):
        return zh if e == 0 else 1 - zh

    def q_send(layer, d, e, dev, idx):
        b = qblk(layer, ring_y[d], zsel(e), c)
        send(b, b, q_s.at[layer, idx], q_r.at[layer, idx], dev)

    def q_got(layer, d, e, idx):
        got(qblk(layer, ring_y[d], zsel(e), c), q_r.at[layer, idx])

    def q_sib(layer, d, e):
        q_send(layer, d, e, dev_sib, 7 + d * 2 + e)

    def q1(layer):
        q_send(layer, 0, 0, dev_z, 0)
        q_send(layer, 0, 0, dev_yp, 1)
        q_send(layer, 0, 0, dev_ym, 3)
        q_sib(layer, 0, 0)

    def q2(layer):
        q_got(layer, 0, 1, 0)
        q_send(layer, 0, 1, dev_yp, 2)
        q_send(layer, 0, 1, dev_ym, 4)
        q_sib(layer, 0, 1)

    def q3(layer):
        q_got(layer, 3, 0, 1)
        q_send(layer, 3, 0, dev_yp, 5)
        q_sib(layer, 3, 0)
        q_got(layer, 1, 0, 3)
        q_sib(layer, 1, 0)
        q_got(layer, 1, 1, 4)
        q_send(layer, 1, 1, dev_ym, 6)
        q_sib(layer, 1, 1)
        q_got(layer, 3, 1, 2)
        q_sib(layer, 3, 1)

    def q4(layer):
        q_got(layer, 2, 0, 5)
        q_sib(layer, 2, 0)
        q_got(layer, 2, 1, 6)
        q_sib(layer, 2, 1)

    def q5(layer):
        for d in range(4):
            for e in range(2):
                got(qblk(layer, ring_y[d], zsel(e), 1 - c), q_r.at[layer, 7 + d * 2 + e])

    def oblk(layer, y_, zh_, core, part=None):
        cols = slice(None) if part is None else pl.ds(part * 1024, 1024)
        return wo.at[layer, core, pl.ds(pl.multiple_of((y_ * 2 + zh_) * 80, 80), 80), cols]

    def o_send(layer, d, e, dev, idx, part=None):
        b = oblk(layer, ring_y[d], zsel(e), c, part)
        send(b, b, o_s.at[layer, idx], o_r.at[layer, idx], dev)

    def o_got(layer, d, e, idx, part=None):
        got(oblk(layer, ring_y[d], zsel(e), c, part), o_r.at[layer, idx])

    def o_pass(layer, d):
        o_send(layer, d, 0, dev_z, 4 + d)
        o_send(layer, d, 0, dev_sib, 8 + d * 2)

    def o1(layer):
        o_send(layer, 0, 0, dev_yp, 0)
        o_send(layer, 0, 0, dev_ym, 1)
        o_pass(layer, 0)

    def o2(layer):
        o_got(layer, 3, 0, 0)
        o_send(layer, 3, 0, dev_yp, 2, 0)
        o_pass(layer, 3)
        o_got(layer, 1, 0, 1)
        o_send(layer, 1, 0, dev_ym, 3, 1)
        o_pass(layer, 1)

    def o3(layer):
        o_got(layer, 2, 0, 2, 0)
        o_got(layer, 2, 0, 3, 1)
        o_pass(layer, 2)

    def o4(layer):
        for d in (0, 3, 1, 2):
            o_got(layer, d, 1, 4 + d)
            o_send(layer, d, 1, dev_sib, 8 + d * 2 + 1)

    def o5(layer):
        for d in range(4):
            for e in range(2):
                got(oblk(layer, ring_y[d], zsel(e), 1 - c), o_r.at[layer, 8 + d * 2 + e])

    ring_x = [x, xp, lax.rem(x + 2, 4), xm]

    def tsel(d, e):
        return ring_x[d] * 2 + (zl if e == 0 else 1 - zl)

    def g_send(n, ref, d, e, dev, idx, own=None):
        b = ref(tsel(d, e))
        send(b if own is None else own, b, g_s.at[n, idx], g_r.at[n, idx], dev)

    def g_got(n, ref, d, e, idx):
        got(ref(tsel(d, e)), g_r.at[n, idx])

    def g1(n, ref, own=None):
        g_send(n, ref, 0, 0, dev_zl, 0, own)
        g_send(n, ref, 0, 0, dev_xp, 1, own)
        g_send(n, ref, 0, 0, dev_xm, 3, own)

    def g2(n, ref):
        g_got(n, ref, 0, 1, 0)
        g_send(n, ref, 0, 1, dev_xp, 2)
        g_send(n, ref, 0, 1, dev_xm, 4)

    def g3(n, ref):
        g_got(n, ref, 3, 0, 1)
        g_send(n, ref, 3, 0, dev_xp, 5)
        g_got(n, ref, 1, 0, 3)
        g_got(n, ref, 1, 1, 4)
        g_send(n, ref, 1, 1, dev_xm, 6)
        g_got(n, ref, 3, 1, 2)

    def g4(n, ref):
        g_got(n, ref, 2, 0, 5)
        g_got(n, ref, 2, 1, 6)

    def normalize(layer, read):
        def body(b, carry):
            rows = pl.ds(pl.multiple_of(b * 32, 32), 32)
            total = jnp.zeros((32, 1), f32)
            for j in range(CHUNKS):
                wide = read(rows, j).astype(f32)
                total = total + jnp.sum(wide * wide, axis=-1, keepdims=True)
            scale = lax.rsqrt(total * (1.0 / D) + epsilon)
            for j in range(CHUNKS):
                norm[j, rows, :] = (read(rows, j).astype(f32) * scale * gain[layer, j]).astype(bf16)
            return carry

        lax.fori_loop(0, FLAT // 32, body, 0)

    def project_in(layer):
        mixed[...] = jnp.zeros_like(mixed)

        def body(j, carry):
            mixed[...] += jnp.dot(norm[j], wq[layer, j], preferred_element_type=f32)
            return carry

        lax.fori_loop(0, CHUNKS, body, 0)

        def turn(v, g):
            n = v * lax.rsqrt(jnp.mean(v * v, axis=-1, keepdims=True) + epsilon) * g
            return n * cosf[...] + pltpu.roll(n, HEAD // 2, 1) * sinf[...]

        for i in range(4):
            q = turn(mixed[:, i * HEAD : (i + 1) * HEAD], qgain[layer])
            for s in range(STEPS):
                qs[(s * 4 + i) * ROWS : (s * 4 + i + 1) * ROWS, :] = q[s * ROWS : (s + 1) * ROWS]
        nk[...] = turn(mixed[:, 4 * HEAD : 5 * HEAD], kgain[layer])
        nv[...] = mixed[:, 5 * HEAD : 6 * HEAD]

    row = lax.broadcasted_iota(jnp.int32, (128, 32), 0)
    col = lax.broadcasted_iota(jnp.int32, (128, 32), 1)
    fresh = jnp.logical_and(
        jnp.right_shift(row, 4) == jnp.bitwise_and(col, 7),
        jnp.right_shift(col, 3) <= jnp.bitwise_and(jnp.right_shift(row, 2), 3),
    )
    slot_index = lax.broadcasted_iota(jnp.int32, (128, SLOTS), 1)

    def attend(layer):
        for copy in kv[layer]:
            copy.wait()

        def body(g, carry):
            q = [qs[pl.ds(g * 8 + k, 16, stride=ROWS), :].astype(bf16) for k in range(8)]
            old = jnp.concatenate(
                [lax.dot_general(q[k], kbuf[g * 8 + k], NT, preferred_element_type=f32) for k in range(8)], axis=0
            ) * HEAD ** (-0.5)
            part = [pl.ds(pl.multiple_of(s * ROWS + g * 8, 8), 8) for s in range(STEPS)]
            keys = jnp.concatenate([nk[w, :] for w in part], axis=0).astype(bf16)
            values = jnp.concatenate([nv[w, :] for w in part], axis=0).astype(bf16)
            new = lax.dot_general(jnp.concatenate(q, axis=0), keys, NT, preferred_element_type=f32) * HEAD ** (-0.5)
            live = slot_index < len16[pl.ds(pl.multiple_of(g * 128, 128), 128), :]
            old = jnp.where(live, old, -jnp.inf)
            new = jnp.where(fresh, new, -jnp.inf)
            top = jnp.maximum(jnp.max(old, axis=-1, keepdims=True), jnp.max(new, axis=-1, keepdims=True))
            old = jnp.exp(old - top)
            new = jnp.exp(new - top)
            below = jnp.sum(old, axis=-1, keepdims=True) + jnp.sum(new, axis=-1, keepdims=True)
            old = (old / below).astype(bf16)
            new = (new / below).astype(bf16)
            fresh_part = jnp.dot(new, values, preferred_element_type=f32)
            for k in range(8):
                rows = slice(k * 16, (k + 1) * 16)
                ao[pl.ds(g * 8 + k, 16, stride=ROWS), :] = (
                    jnp.dot(old[rows], vbuf[g * 8 + k], preferred_element_type=f32) + fresh_part[rows]
                )
            return carry

        lax.fori_loop(0, ROWS // 8, body, 0)
        for s in range(STEPS):
            for i in range(4):
                att[layer, t, s * ROWS : (s + 1) * ROWS, i * HEAD : (i + 1) * HEAD] = ao[
                    (s * 4 + i) * ROWS : (s * 4 + i + 1) * ROWS, :
                ].astype(bf16)

    def project_out(layer, before):
        total = before.astype(f32)
        part = jnp.zeros((FLAT, CHUNK), f32)
        for k in range(TP):
            part = part + lax.dot_general(
                att[layer, k], wo[layer, k // 4, :, (k % 4) * ATT : (k % 4 + 1) * ATT], NT, preferred_element_type=f32
            )
        return (total + part).astype(bf16)

    def att_ref(layer):
        return lambda k: att.at[layer, k]

    def hid_ref(k):
        return hid.at[k]

    def out_ref(k):
        return out.at[k]

    start_exchange()
    start_second()
    load_x.wait()
    normalize(0, lambda rows, j: xin[rows, j * CHUNK : (j + 1) * CHUNK])
    pack_q(0)
    q1(0)
    pack_o(0)
    q2(0)
    pack_o(1)
    pack_q(1)
    q3(0)
    o1(0)
    q4(0)
    q5(0)
    project_in(0)
    o2(0)
    q1(1)
    attend(0)
    load_kv(1)
    o3(0)
    g1(0, att_ref(0))
    q2(1)
    g2(0, att_ref(0))
    o4(0)
    q3(1)
    g3(0, att_ref(0))
    o1(1)
    o5(0)
    g4(0, att_ref(0))
    hid[t] = project_out(0, resid[...])
    g1(1, hid_ref)
    q4(1)
    o2(1)
    g2(1, hid_ref)
    q5(1)
    o3(1)
    g3(1, hid_ref)
    o4(1)
    g4(1, hid_ref)
    normalize(1, lambda rows, j: hid[j, rows, :])
    project_in(1)
    attend(1)
    g1(2, att_ref(1))
    g2(2, att_ref(1))
    g3(2, att_ref(1))
    o5(1)
    g4(2, att_ref(1))
    hown[...] = project_out(1, hid[t])
    keep = pltpu.make_async_copy(hown, out.at[t], loc.at[3])
    keep.start()
    g1(3, out_ref, hown)
    g2(3, out_ref)
    g3(3, out_ref)
    g4(3, out_ref)
    keep.wait()
    for copy in sent:
        copy.wait_send()

    @pl.when(half_of_t != c)
    def _():
        sibling_slab().wait_send()


def fused(*operands):
    whole = pl.BlockSpec(memory_space=pltpu.VMEM)
    anywhere = pl.BlockSpec(memory_space=pl.ANY)
    dma = pltpu.SemaphoreType.DMA
    return pl.pallas_call(
        kernel,
        out_shape=jax.ShapeDtypeStruct((TP, FLAT, CHUNK), bf16),
        in_specs=[anywhere] * 3 + [whole] * 7 + [anywhere] * 2,
        out_specs=anywhere,
        scratch_shapes=[
            pltpu.VMEM((LAYERS, CHUNKS, CHUNK, GROUP), bf16),
            pltpu.VMEM((LAYERS, 2, CHUNK, HALF), bf16),
            pltpu.VMEM((LAYERS, TP, PAD, GROUP), bf16),
            pltpu.VMEM((LAYERS, 2, PAD, HALF), bf16),
            pltpu.VMEM((TP * OWN, GROUP), f32),
            pltpu.VMEM((FLAT, D), bf16),
            pltpu.VMEM((CHUNKS, FLAT, CHUNK), bf16),
            pltpu.VMEM((TP, FLAT, CHUNK), bf16),
            pltpu.VMEM((FLAT, CHUNK), bf16),
            pltpu.VMEM((LAYERS, TP, FLAT, ATT), bf16),
            pltpu.VMEM((ROWS, SLOTS, HEAD), bf16),
            pltpu.VMEM((ROWS, SLOTS, HEAD), bf16),
            pltpu.VMEM((16 * ROWS, HEAD), f32),
            pltpu.VMEM((16 * ROWS, HEAD), f32),
            pltpu.VMEM((FLAT, HEAD), f32),
            pltpu.VMEM((FLAT, HEAD), f32),
            pltpu.VMEM((FLAT, GROUP), f32),
            dma((LAYERS, TP)), dma((LAYERS, TP)),
            dma((LAYERS,)), dma((LAYERS, 3)),
            dma((LAYERS, 15)), dma((LAYERS, 15)),
            dma((LAYERS, 16)), dma((LAYERS, 16)),
            dma((4, 7)), dma((4, 7)),
            dma((4,)),
        ],
        compiler_params=pltpu.CompilerParams(
            collective_id=0, has_side_effects=True, vmem_limit_bytes=60 * 1024 * 1024
        ),
    )(*operands)


def on_device(
    inputs, qkv_weight, out_weight, norm_gain, query_gain, key_gain, stored_rotated_keys, stored_cache_values, lengths
):
    t = lax.axis_index("tp")
    flat = inputs.reshape(FLAT, D)
    resid = lax.dynamic_slice_in_dim(flat.reshape(FLAT, 16, TP * OWN), t * OWN, OWN, axis=2).reshape(FLAT, CHUNK)
    qw = jnp.pad(qkv_weight, ((0, 0), (0, PAD - OWN), (0, 0)))
    ow = jnp.pad(out_weight, ((0, 0), (0, PAD - OWN), (0, 0)))
    second = norm_gain[1].reshape(16, TP, OWN).transpose(1, 0, 2).reshape(D)
    gain = jnp.stack([norm_gain[0], second]).reshape(LAYERS, CHUNKS, 1, CHUNK)
    positions = lengths[None, :] + jnp.arange(STEPS, dtype=jnp.int32)[:, None]
    half = HEAD // 2
    frequency = rope_base ** (-jnp.arange(half, dtype=f32) / half)
    angles = (positions.astype(f32)[..., None] * frequency).reshape(FLAT, half)
    cosine, sine = jnp.cos(angles), jnp.sin(angles)
    cosf = jnp.concatenate([cosine, cosine], axis=-1)
    sinf = jnp.concatenate([-sine, sine], axis=-1)
    len16 = jnp.repeat(lengths, 16).reshape(ROWS * 16, 1)
    hidden = fused(
        flat, qw, ow, resid, gain, query_gain.reshape(LAYERS, 1, HEAD), key_gain.reshape(LAYERS, 1, HEAD),
        cosf, sinf, len16,
        stored_rotated_keys.reshape(LAYERS, ROWS, SLOTS, HEAD), stored_cache_values.reshape(LAYERS, ROWS, SLOTS, HEAD),
    )
    natural = hidden.reshape(TP, FLAT, 16, OWN).transpose(1, 2, 0, 3)
    return natural.reshape(STEPS, ROWS, D)


def solution(mesh):
    return jax.shard_map(
        on_device,
        mesh=mesh,
        in_specs=(
            P(None, "rep", None),
            P(None, ("rep", "tp"), None),
            P(None, ("rep", "tp"), None),
            P(),
            P(),
            P(),
            P(None, "rep", "tp", None, None),
            P(None, "rep", "tp", None, None),
            P("rep"),
        ),
        out_specs=P(None, "rep", None),
        check_vma=False,
    )
```

```python
import functools

import jax
import jax.numpy as jnp
from jax import lax
from jax.experimental import pallas as pl
from jax.experimental.pallas import tpu as pltpu
from jax.sharding import PartitionSpec as P

MESH = pl.DeviceIdType.MESH
epsilon = 1e-06
rope_base = 1000000.0

LAYERS = 2
STEPS = 4
ROWS = 64
FLAT = STEPS * ROWS
PARTS = 2
SIDE = ROWS // PARTS
PART = FLAT // PARTS
D = 5120
CHUNKS = 8
CHUNK = D // CHUNKS
OWN = 40
PAD = 48
HEAD = 128
GROUP = 768
ATT = 512
SLOTS = 256
HALF = 2048
TP = 8
f32 = jnp.float32
bf16 = jnp.bfloat16

NT = (((1,), (1,)), ((), ()))


def kernel(
    x_hbm, qw, ow, gains, qgain, kgain, rows_len, frequency, k_hbm, v_hbm,
    out,
    wq, wo, land_q, land_o, pack, xin, norm, hid, hown, att, kbuf, vbuf, qs, ao, nk, nv, mixed, resid, gain, cosf, sinf, limit,
    a2a_s, a2a_r, ex_s, ex_r, q_s, q_r, o_s, o_r, g_s, g_r, loc,
):
    r = lax.axis_index("rep")
    t = lax.axis_index("tp")
    y = lax.div(r, 4)
    zh = lax.rem(lax.div(r, 2), 2)
    c = lax.rem(r, 2)
    p = lax.div(r, 2)
    x = lax.div(t, 2)
    zl = lax.rem(t, 2)

    def rep(y_, zh_, c_):
        return y_ * 4 + zh_ * 2 + c_

    yp, ym, y2 = lax.rem(y + 1, 4), lax.rem(y + 3, 4), lax.rem(y + 2, 4)
    xp, xm = lax.rem(x + 1, 4), lax.rem(x + 3, 4)
    dev_yp = (rep(yp, zh, c), t)
    dev_ym = (rep(ym, zh, c), t)
    dev_z = (rep(y, 1 - zh, c), t)
    dev_sib = (rep(y, zh, 1 - c), t)
    dev_xp = (r, xp * 2 + zl)
    dev_xm = (r, xm * 2 + zl)
    dev_zl = (r, x * 2 + 1 - zl)

    sent = []

    def send(src, dst, ss, rs, dev):
        copy = pltpu.make_async_remote_copy(
            src_ref=src, dst_ref=dst, send_sem=ss, recv_sem=rs, device_id=dev, device_id_type=MESH
        )
        copy.start()
        sent.append(copy)

    def got(ref, rs):
        pltpu.make_async_remote_copy(
            src_ref=ref, dst_ref=ref, send_sem=rs, recv_sem=rs, device_id=dev_sib, device_id_type=MESH
        ).wait_recv()

    barrier = pltpu.get_barrier_semaphore()
    greet = [dev_yp, dev_ym, dev_z, dev_sib]
    for k in range(1, TP):
        other = lax.rem(t + k, TP)
        greet.append((r, other))
        greet.append((rep(y, zh, 1 - c), other))
    for dev in greet:
        pl.semaphore_signal(barrier, inc=1, device_id=dev, device_id_type=MESH)
    pl.semaphore_wait(barrier, len(greet))

    load_x = [
        pltpu.make_async_copy(
            x_hbm.at[s, pl.ds(h * SIDE, SIDE)], xin.at[pl.ds(h * PART + s * SIDE, SIDE)], loc.at[4 + h * STEPS + s]
        )
        for h in range(PARTS)
        for s in range(STEPS)
    ]
    for copy in load_x:
        copy.start()
    kv = {}

    def load_kv(layer):
        kv[layer] = [
            pltpu.make_async_copy(k_hbm.at[layer], kbuf, loc.at[1]),
            pltpu.make_async_copy(v_hbm.at[layer], vbuf, loc.at[2]),
        ]
        for copy in kv[layer]:
            copy.start()

    def qcols(other):
        return pl.ds(pl.multiple_of(other * GROUP, GROUP), GROUP)

    slab = first, second = pl.ds(0, PAD), pl.ds(2 * OWN - PAD, PAD)
    skip = (0, PAD - OWN)
    half_of_t = lax.div(t, 4)
    slot1 = lax.rem(t, 4) * 2 + c
    for k in range(1, TP):
        other = lax.rem(t + k, TP)
        send(qw.at[first, qcols(other)], land_q.at[0, t], a2a_s.at[0, k], a2a_r.at[0, t], (r, other))
    own0 = pltpu.make_async_copy(qw.at[first, qcols(t)], land_q.at[0, t], a2a_r.at[0, t])
    own0.start()
    load_kv(0)

    def start_exchange():
        for layer in range(LAYERS):
            theirs = pl.ds(pl.multiple_of((1 - c) * HALF, HALF), HALF)
            mine = pl.ds(pl.multiple_of(c * HALF, HALF), HALF)
            send(ow.at[slab[layer], theirs], land_o.at[layer, c], ex_s.at[layer], ex_r.at[layer, c], dev_sib)
            pltpu.make_async_copy(ow.at[slab[layer], mine], land_o.at[layer, c], ex_r.at[layer, 2]).start()

    def sibling_slab():
        return pltpu.make_async_remote_copy(
            src_ref=qw.at[second, qcols(t)], dst_ref=land_q.at[1, slot1], send_sem=a2a_s.at[1, 0],
            recv_sem=a2a_r.at[1, slot1], device_id=dev_sib, device_id_type=MESH,
        )

    def start_second():
        for k in range(1, TP):
            other = lax.rem(t + k, TP)
            send(
                qw.at[second, qcols(other)], land_q.at[1, slot1], a2a_s.at[1, k], a2a_r.at[1, slot1],
                (rep(y, zh, half_of_t), other),
            )

        @pl.when(half_of_t == c)
        def _():
            pltpu.make_async_copy(qw.at[second, qcols(t)], land_q.at[1, slot1], a2a_r.at[1, slot1]).start()

        @pl.when(half_of_t != c)
        def _():
            sibling_slab().start()

    def pack_q(layer):
        for slot in range(TP):
            got(land_q.at[layer, slot], a2a_r.at[layer, slot])
        for slot in range(TP):
            pack[slot * OWN : (slot + 1) * OWN, :] = land_q[layer, slot].astype(f32)[skip[layer] : skip[layer] + OWN]
        if layer == 0:
            wq[0, p, pl.ds(pl.multiple_of(c * 320, 320), 320), :] = pack[...].astype(bf16)
        else:
            for k in range(4):
                wq[1, 4 * c + k, pl.ds(pl.multiple_of(p * 80, 80), 80), :] = pack[k * 80 : (k + 1) * 80, :].astype(bf16)

    def pack_o(layer):
        pltpu.make_async_copy(ow.at[slab[layer], pl.ds(0, HALF)], land_o.at[layer, c], ex_r.at[layer, 2]).wait()
        got(land_o.at[layer, 1 - c], ex_r.at[layer, 1 - c])
        for cut in range(4):
            cols = slice(cut * 512, (cut + 1) * 512)
            both = jnp.concatenate(
                [land_o[layer, core, :, cols].astype(f32)[skip[layer] : skip[layer] + OWN] for core in range(2)], axis=0
            )
            wo[layer, c, pl.ds(pl.multiple_of(p * 80, 80), 80), cols] = both.astype(bf16)

    def qblk(layer, y_, zh_, core):
        if layer == 0:
            return wq.at[0, y_ * 2 + zh_, pl.ds(pl.multiple_of(core * 320, 320), 320), :]
        return wq.at[1, pl.ds(4 * core, 4), pl.ds(pl.multiple_of((y_ * 2 + zh_) * 80, 80), 80), :]

    ring_y = [y, yp, y2, ym]

    def zsel(e):
        return zh if e == 0 else 1 - zh

    def q_send(layer, d, e, dev, idx):
        b = qblk(layer, ring_y[d], zsel(e), c)
        send(b, b, q_s.at[layer, idx], q_r.at[layer, idx], dev)

    def q_got(layer, d, e, idx):
        got(qblk(layer, ring_y[d], zsel(e), c), q_r.at[layer, idx])

    def q_sib(layer, d, e):
        q_send(layer, d, e, dev_sib, 7 + d * 2 + e)

    def q1(layer):
        q_send(layer, 0, 0, dev_z, 0)
        q_send(layer, 0, 0, dev_yp, 1)
        q_send(layer, 0, 0, dev_ym, 3)
        q_sib(layer, 0, 0)

    def q2(layer):
        q_got(layer, 0, 1, 0)
        q_send(layer, 0, 1, dev_yp, 2)
        q_send(layer, 0, 1, dev_ym, 4)
        q_sib(layer, 0, 1)

    def q3(layer):
        q_got(layer, 3, 0, 1)
        q_send(layer, 3, 0, dev_yp, 5)
        q_sib(layer, 3, 0)
        q_got(layer, 1, 0, 3)
        q_sib(layer, 1, 0)
        q_got(layer, 1, 1, 4)
        q_send(layer, 1, 1, dev_ym, 6)
        q_sib(layer, 1, 1)
        q_got(layer, 3, 1, 2)
        q_sib(layer, 3, 1)

    def q4(layer):
        q_got(layer, 2, 0, 5)
        q_sib(layer, 2, 0)
        q_got(layer, 2, 1, 6)
        q_sib(layer, 2, 1)

    def q5(layer):
        for d in range(4):
            for e in range(2):
                got(qblk(layer, ring_y[d], zsel(e), 1 - c), q_r.at[layer, 7 + d * 2 + e])

    def oblk(layer, y_, zh_, core, part=None):
        cols = slice(None) if part is None else pl.ds(part * 1024, 1024)
        return wo.at[layer, core, pl.ds(pl.multiple_of((y_ * 2 + zh_) * 80, 80), 80), cols]

    def o_send(layer, d, e, dev, idx, part=None):
        b = oblk(layer, ring_y[d], zsel(e), c, part)
        send(b, b, o_s.at[layer, idx], o_r.at[layer, idx], dev)

    def o_got(layer, d, e, idx, part=None):
        got(oblk(layer, ring_y[d], zsel(e), c, part), o_r.at[layer, idx])

    def o_pass(layer, d):
        o_send(layer, d, 0, dev_z, 4 + d)
        o_send(layer, d, 0, dev_sib, 8 + d * 2)

    def o1(layer):
        o_send(layer, 0, 0, dev_yp, 0)
        o_send(layer, 0, 0, dev_ym, 1)
        o_pass(layer, 0)

    def o2(layer):
        o_got(layer, 3, 0, 0)
        o_send(layer, 3, 0, dev_yp, 2, 0)
        o_pass(layer, 3)
        o_got(layer, 1, 0, 1)
        o_send(layer, 1, 0, dev_ym, 3, 1)
        o_pass(layer, 1)

    def o3(layer):
        o_got(layer, 2, 0, 2, 0)
        o_got(layer, 2, 0, 3, 1)
        o_pass(layer, 2)

    def o4(layer):
        for d in (0, 3, 1, 2):
            o_got(layer, d, 1, 4 + d)
            o_send(layer, d, 1, dev_sib, 8 + d * 2 + 1)

    def o5(layer):
        for d in range(4):
            for e in range(2):
                got(oblk(layer, ring_y[d], zsel(e), 1 - c), o_r.at[layer, 8 + d * 2 + e])

    ring_x = [x, xp, lax.rem(x + 2, 4), xm]

    def tsel(d, e):
        return ring_x[d] * 2 + (zl if e == 0 else 1 - zl)

    def g_send(n, ref, d, e, dev, idx, own=None):
        b = ref(tsel(d, e))
        send(b if own is None else own, b, g_s.at[n, idx], g_r.at[n, idx], dev)

    def g_got(n, ref, d, e, idx):
        got(ref(tsel(d, e)), g_r.at[n, idx])

    def g1(n, ref, own=None):
        g_send(n, ref, 0, 0, dev_zl, 0, own)
        g_send(n, ref, 0, 0, dev_xp, 1, own)
        g_send(n, ref, 0, 0, dev_xm, 3, own)

    def g2(n, ref):
        g_got(n, ref, 0, 1, 0)
        g_send(n, ref, 0, 1, dev_xp, 2)
        g_send(n, ref, 0, 1, dev_xm, 4)

    def g3(n, ref):
        g_got(n, ref, 3, 0, 1)
        g_send(n, ref, 3, 0, dev_xp, 5)
        g_got(n, ref, 1, 0, 3)
        g_got(n, ref, 1, 1, 4)
        g_send(n, ref, 1, 1, dev_xm, 6)
        g_got(n, ref, 3, 1, 2)

    def g4(n, ref):
        g_got(n, ref, 2, 0, 5)
        g_got(n, ref, 2, 1, 6)

    def prepare():
        diagonal = lax.broadcasted_iota(jnp.int32, (ROWS, ROWS), 0) == lax.broadcasted_iota(jnp.int32, (ROWS, ROWS), 1)
        length = jnp.sum(
            jnp.where(diagonal, jnp.broadcast_to(rows_len[...].astype(f32), (ROWS, ROWS)), 0.0), axis=1, keepdims=True
        )
        limit[...] = jnp.broadcast_to(length, (ROWS, SLOTS))
        flip = jnp.where(lax.broadcasted_iota(jnp.int32, (1, HEAD), 1) < HEAD // 2, -1.0, 1.0)
        for h in range(PARTS):
            for s in range(STEPS):
                angles = (length[h * SIDE : (h + 1) * SIDE] + float(s)) * frequency[...]
                rows = slice(h * PART + s * SIDE, h * PART + (s + 1) * SIDE)
                cosf[rows, :] = jnp.cos(angles)
                sinf[rows, :] = jnp.sin(angles) * flip
        for j in range(CHUNKS):
            gain[j : j + 1, :] = gains[0:1, j * CHUNK : (j + 1) * CHUNK]
            gain[CHUNKS + j : CHUNKS + j + 1, :] = jnp.concatenate(
                [gains[1:2, k * 320 + j * OWN : k * 320 + (j + 1) * OWN] for k in range(16)], axis=1
            )

    def pick_own():
        src = lax.broadcasted_iota(jnp.int32, (CHUNK, 256), 0)
        dst = lax.broadcasted_iota(jnp.int32, (CHUNK, 256), 1)
        for j in range(CHUNKS):
            base, shift = j * 80 // 128 * 128, j * 80 % 128
            place = dst - shift
            wanted = jnp.where(place < OWN, place + t * OWN, place + (320 - OWN) + t * OWN)
            ok = jnp.logical_and(jnp.logical_and(place >= 0, place < 2 * OWN), src == wanted)
            pick = jnp.where(ok, 1.0, 0.0).astype(bf16)
            mine = jnp.dot(xin[:, j * CHUNK : (j + 1) * CHUNK], pick, preferred_element_type=f32)
            width = min(256, CHUNK - base)
            if j == 0:
                resid[...] = jnp.zeros_like(resid)
            resid[:, base : base + width] += mine[:, :width]

    def normalize(layer, start, count, read):
        def body(b, carry):
            rows = pl.ds(pl.multiple_of(b * 32, 32), 32)
            inside = pl.ds(pl.multiple_of(b * 32 - start, 32), 32)
            total = jnp.zeros((32, 1), f32)
            for j in range(CHUNKS):
                wide = read(inside, j).astype(f32)
                total = total + jnp.sum(wide * wide, axis=-1, keepdims=True)
            scale = lax.rsqrt(total * (1.0 / D) + epsilon)
            for j in range(CHUNKS):
                norm[j, rows, :] = (read(inside, j).astype(f32) * scale * gain[layer * CHUNKS + j : layer * CHUNKS + j + 1, :]).astype(bf16)
            return carry

        lax.fori_loop(start // 32, (start + count) // 32, body, 0)

    def project_in(layer, start, count):
        rows = slice(start, start + count)
        mixed[rows, :] = jnp.zeros((count, GROUP), f32)

        def body(j, carry):
            mixed[rows, :] += jnp.dot(norm[j, rows], wq[layer, j], preferred_element_type=f32)
            return carry

        lax.fori_loop(0, CHUNKS, body, 0)

        def turn(v, g):
            n = v * lax.rsqrt(jnp.mean(v * v, axis=-1, keepdims=True) + epsilon) * g
            return n * cosf[rows, :] + pltpu.roll(n, HEAD // 2, 1) * sinf[rows, :]

        for i in range(4):
            q = turn(mixed[rows, i * HEAD : (i + 1) * HEAD], qgain[layer])
            for h in range(start // PART, (start + count) // PART):
                for s in range(STEPS):
                    at = h * PART + s * SIDE - start
                    to = (s * 4 + i) * ROWS + h * SIDE
                    qs[to : to + SIDE, :] = q[at : at + SIDE]
        nk[rows, :] = turn(mixed[rows, 4 * HEAD : 5 * HEAD], kgain[layer])
        nv[rows, :] = mixed[rows, 5 * HEAD : 6 * HEAD]

    row = lax.broadcasted_iota(jnp.int32, (128, 32), 0)
    col = lax.broadcasted_iota(jnp.int32, (128, 32), 1)
    fresh = jnp.logical_and(
        jnp.right_shift(row, 4) == jnp.bitwise_and(col, 7),
        jnp.right_shift(col, 3) <= jnp.bitwise_and(jnp.right_shift(row, 2), 3),
    )
    slot_index = lax.broadcasted_iota(jnp.int32, (16, SLOTS), 1).astype(f32)

    def attend(layer, h):
        if h == 0:
            for copy in kv[layer]:
                copy.wait()

        def body(g, carry):
            q = [qs[pl.ds(g * 8 + k, 16, stride=ROWS), :].astype(bf16) for k in range(8)]
            old = []
            for k in range(8):
                score = lax.dot_general(q[k], kbuf[g * 8 + k], NT, preferred_element_type=f32) * HEAD ** (-0.5)
                old.append(jnp.where(slot_index < limit[pl.ds(g * 8 + k, 1), :], score, -jnp.inf))
            old = jnp.concatenate(old, axis=0)
            part = [pl.ds(pl.multiple_of(h * (PART - SIDE) + s * SIDE + g * 8, 8), 8) for s in range(STEPS)]
            keys = jnp.concatenate([nk[w, :] for w in part], axis=0).astype(bf16)
            values = jnp.concatenate([nv[w, :] for w in part], axis=0).astype(bf16)
            new = lax.dot_general(jnp.concatenate(q, axis=0), keys, NT, preferred_element_type=f32) * HEAD ** (-0.5)
            new = jnp.where(fresh, new, -jnp.inf)
            top = jnp.maximum(jnp.max(old, axis=-1, keepdims=True), jnp.max(new, axis=-1, keepdims=True))
            old = jnp.exp(old - top)
            new = jnp.exp(new - top)
            below = jnp.sum(old, axis=-1, keepdims=True) + jnp.sum(new, axis=-1, keepdims=True)
            old = (old / below).astype(bf16)
            new = (new / below).astype(bf16)
            fresh_part = jnp.dot(new, values, preferred_element_type=f32)
            for k in range(8):
                rows = slice(k * 16, (k + 1) * 16)
                ao[pl.ds(g * 8 + k, 16, stride=ROWS), :] = (
                    jnp.dot(old[rows], vbuf[g * 8 + k], preferred_element_type=f32) + fresh_part[rows]
                )
            return carry

        lax.fori_loop(h * SIDE // 8, (h + 1) * SIDE // 8, body, 0)
        for s in range(STEPS):
            for i in range(4):
                start = (s * 4 + i) * ROWS + h * SIDE
                att[layer, h, t, s * SIDE : (s + 1) * SIDE, i * HEAD : (i + 1) * HEAD] = ao[
                    start : start + SIDE, :
                ].astype(bf16)

    def project_out(layer, h, before):
        total = jnp.zeros((PART, CHUNK), f32)
        for k in range(TP):
            total = total + lax.dot_general(
                att[layer, h, k], wo[layer, k // 4, :, (k % 4) * ATT : (k % 4 + 1) * ATT], NT,
                preferred_element_type=f32,
            )
        return (before.astype(f32) + total).astype(bf16)

    def att_ref(layer, h):
        return lambda k: att.at[layer, h, k]

    def hid_ref(h):
        return lambda k: hid.at[h, k]

    def out_ref(h):
        return lambda k: out.at[h, k]

    refs = [
        att_ref(0, 0), att_ref(0, 1), hid_ref(0), hid_ref(1), att_ref(1, 0), att_ref(1, 1), out_ref(0), out_ref(1)
    ]

    def g(step, n, own=None):
        if step == 1:
            g1(n, refs[n], own)
        else:
            (g2, g3, g4)[step - 2](n, refs[n])

    def first_out(h):
        hid[h, t] = project_out(0, h, resid[h * PART : (h + 1) * PART, :])
        g(1, 2 + h)

    def second_in(h):
        normalize(1, h * PART, PART, lambda rows, j: hid[h, j, rows, :])
        project_in(1, h * PART, PART)
        attend(1, h)
        g(1, 4 + h)

    keep = [pltpu.make_async_copy(hown.at[h], out.at[h, t], loc.at[3 * h]) for h in range(PARTS)]

    def second_out(h):
        hown[h] = project_out(1, h, hid[h, t])
        g(1, 6 + h, hown.at[h])
        keep[h].start()

    start_exchange()
    prepare()
    pack_o(0)
    o1(0)
    for copy in load_x:
        copy.wait()
    pick_own()
    normalize(0, 0, FLAT, lambda rows, j: xin[rows, j * CHUNK : (j + 1) * CHUNK])
    pack_q(0)
    q1(0)
    start_second()
    pack_o(1)
    q2(0)
    o2(0)
    q3(0)
    pack_q(1)
    q1(1)
    o3(0)
    q4(0)
    q5(0)
    project_in(0, 0, FLAT)
    attend(0, 0)
    g(1, 0)
    attend(0, 1)
    g(1, 1)
    load_kv(1)
    g(2, 0)
    q2(1)
    g(2, 1)
    g(3, 0)
    o4(0)
    o5(0)
    g(3, 1)
    g(4, 0)
    first_out(0)
    q3(1)
    g(4, 1)
    first_out(1)
    o1(1)
    g(2, 2)
    g(2, 3)
    g(3, 2)
    q4(1)
    q5(1)
    g(4, 2)
    o2(1)
    second_in(0)
    g(3, 3)
    g(4, 3)
    second_in(1)
    g(2, 4)
    g(2, 5)
    g(3, 4)
    o3(1)
    o4(1)
    g(3, 5)
    o5(1)
    g(4, 4)
    second_out(0)
    g(4, 5)
    second_out(1)
    g(2, 6)
    g(2, 7)
    g(3, 6)
    g(3, 7)
    g(4, 6)
    g(4, 7)
    for copy in keep:
        copy.wait()
    for copy in sent:
        copy.wait_send()

    @pl.when(half_of_t != c)
    def _():
        sibling_slab().wait_send()


def fused(*operands):
    whole = pl.BlockSpec(memory_space=pltpu.VMEM)
    anywhere = pl.BlockSpec(memory_space=pl.ANY)
    dma = pltpu.SemaphoreType.DMA
    return pl.pallas_call(
        kernel,
        out_shape=jax.ShapeDtypeStruct((PARTS, TP, PART, CHUNK), bf16),
        in_specs=[anywhere] * 3 + [whole] * 5 + [anywhere] * 2,
        out_specs=anywhere,
        scratch_shapes=[
            pltpu.VMEM((LAYERS, CHUNKS, CHUNK, GROUP), bf16),
            pltpu.VMEM((LAYERS, 2, CHUNK, HALF), bf16),
            pltpu.VMEM((LAYERS, TP, PAD, GROUP), bf16),
            pltpu.VMEM((LAYERS, 2, PAD, HALF), bf16),
            pltpu.VMEM((TP * OWN, GROUP), f32),
            pltpu.VMEM((FLAT, D), bf16),
            pltpu.VMEM((CHUNKS, FLAT, CHUNK), bf16),
            pltpu.VMEM((PARTS, TP, PART, CHUNK), bf16),
            pltpu.VMEM((PARTS, PART, CHUNK), bf16),
            pltpu.VMEM((LAYERS, PARTS, TP, PART, ATT), bf16),
            pltpu.VMEM((ROWS, SLOTS, HEAD), bf16),
            pltpu.VMEM((ROWS, SLOTS, HEAD), bf16),
            pltpu.VMEM((16 * ROWS, HEAD), f32),
            pltpu.VMEM((16 * ROWS, HEAD), f32),
            pltpu.VMEM((FLAT, HEAD), f32),
            pltpu.VMEM((FLAT, HEAD), f32),
            pltpu.VMEM((FLAT, GROUP), f32),
            pltpu.VMEM((FLAT, CHUNK), f32),
            pltpu.VMEM((LAYERS * CHUNKS, CHUNK), f32),
            pltpu.VMEM((FLAT, HEAD), f32),
            pltpu.VMEM((FLAT, HEAD), f32),
            pltpu.VMEM((ROWS, SLOTS), f32),
            dma((LAYERS, TP)), dma((LAYERS, TP)),
            dma((LAYERS,)), dma((LAYERS, 3)),
            dma((LAYERS, 15)), dma((LAYERS, 15)),
            dma((LAYERS, 16)), dma((LAYERS, 16)),
            dma((4 * PARTS, 7)), dma((4 * PARTS, 7)),
            dma((4 + PARTS * STEPS,)),
        ],
        compiler_params=pltpu.CompilerParams(
            collective_id=0, has_side_effects=True, vmem_limit_bytes=60 * 1024 * 1024
        ),
    )(*operands)


def restore_kernel(hidden, natural):
    for p in range(CHUNKS):
        window = slice(p * 80 // 128 * 128, -(-(p + 1) * 80 // 128) * 128)
        wide = [hidden[0, k, :, window].astype(f32) for k in range(TP)]
        start = p * 80 % 128
        parts = [wide[k][:, start + core * OWN : start + (core + 1) * OWN] for core in range(2) for k in range(TP)]
        natural[0, :, p * CHUNK : (p + 1) * CHUNK] = jnp.concatenate(parts, axis=1).astype(bf16)


def restore(hidden):
    return pl.pallas_call(
        restore_kernel,
        out_shape=jax.ShapeDtypeStruct((STEPS, ROWS, D), bf16),
        grid=(PARTS, STEPS),
        in_specs=[pl.BlockSpec((1, TP, SIDE, CHUNK), lambda h, s: (h, 0, s, 0))],
        out_specs=pl.BlockSpec((1, SIDE, D), lambda h, s: (s, h, 0)),
        compiler_params=pltpu.CompilerParams(vmem_limit_bytes=32 * 1024 * 1024),
    )(hidden)


def on_device(
    inputs, qkv_weight, out_weight, norm_gain, query_gain, key_gain, stored_rotated_keys, stored_cache_values, lengths
):
    half = HEAD // 2
    frequency = rope_base ** (-jnp.arange(half, dtype=f32) / half)
    hidden = fused(
        inputs,
        qkv_weight.reshape(LAYERS * OWN, TP * GROUP),
        out_weight.reshape(LAYERS * OWN, TP * ATT),
        norm_gain,
        query_gain.reshape(LAYERS, 1, HEAD),
        key_gain.reshape(LAYERS, 1, HEAD),
        lengths.reshape(1, ROWS),
        jnp.concatenate([frequency, frequency]).reshape(1, HEAD),
        stored_rotated_keys.reshape(LAYERS, ROWS, SLOTS, HEAD),
        stored_cache_values.reshape(LAYERS, ROWS, SLOTS, HEAD),
    )
    return restore(hidden)


def solution(mesh):
    return jax.shard_map(
        on_device,
        mesh=mesh,
        in_specs=(
            P(None, "rep", None),
            P(None, ("rep", "tp"), None),
            P(None, ("rep", "tp"), None),
            P(),
            P(),
            P(),
            P(None, "rep", "tp", None, None),
            P(None, "rep", "tp", None, None),
            P("rep"),
        ),
        out_specs=P(None, "rep", None),
        check_vma=False,
    )
```

```python
import functools

import jax
import jax.numpy as jnp
from jax import lax
from jax.experimental import pallas as pl
from jax.experimental.pallas import tpu as pltpu
from jax.sharding import PartitionSpec as P

MESH = pl.DeviceIdType.MESH
epsilon = 1e-06
rope_base = 1000000.0

LAYERS = 2
STEPS = 4
ROWS = 64
FLAT = STEPS * ROWS
PARTS = 2
SIDE = ROWS // PARTS
PART = FLAT // PARTS
D = 5120
CHUNKS = 8
CHUNK = D // CHUNKS
OWN = 40
PAD = 48
HEAD = 128
GROUP = 768
ATT = 512
SLOTS = 256
HALF = 2048
TP = 8
f32 = jnp.float32
bf16 = jnp.bfloat16

O_Z_FIRST = (True, True)
G_Z_FIRST = (True, False, True, False, True, False, True, False)
NT = (((1,), (1,)), ((), ()))


def kernel(
    x_hbm, qw, ow, gains, qgain, kgain, rows_len, frequency, k_hbm, v_hbm,
    out,
    wq, wo, land_q, land_o, pack, xin, norm, hid, hown, att, kbuf, vbuf, qs, ao, nk, nv, mixed, resid, gain, cosf, sinf, limit,
    a2a_s, a2a_r, ex_s, ex_r, q_s, q_r, o_s, o_r, g_s, g_r, loc,
):
    r = lax.axis_index("rep")
    t = lax.axis_index("tp")
    y = lax.div(r, 4)
    zh = lax.rem(lax.div(r, 2), 2)
    c = lax.rem(r, 2)
    p = lax.div(r, 2)
    x = lax.div(t, 2)
    zl = lax.rem(t, 2)

    def rep(y_, zh_, c_):
        return y_ * 4 + zh_ * 2 + c_

    yp, ym, y2 = lax.rem(y + 1, 4), lax.rem(y + 3, 4), lax.rem(y + 2, 4)
    xp, xm = lax.rem(x + 1, 4), lax.rem(x + 3, 4)
    dev_yp = (rep(yp, zh, c), t)
    dev_ym = (rep(ym, zh, c), t)
    dev_z = (rep(y, 1 - zh, c), t)
    dev_sib = (rep(y, zh, 1 - c), t)
    dev_xp = (r, xp * 2 + zl)
    dev_xm = (r, xm * 2 + zl)
    dev_zl = (r, x * 2 + 1 - zl)

    sent = []

    def send(src, dst, ss, rs, dev):
        copy = pltpu.make_async_remote_copy(
            src_ref=src, dst_ref=dst, send_sem=ss, recv_sem=rs, device_id=dev, device_id_type=MESH
        )
        copy.start()
        sent.append(copy)

    def got(ref, rs):
        pltpu.make_async_remote_copy(
            src_ref=ref, dst_ref=ref, send_sem=rs, recv_sem=rs, device_id=dev_sib, device_id_type=MESH
        ).wait_recv()

    barrier = pltpu.get_barrier_semaphore()
    greet = [dev_yp, dev_ym, dev_z, dev_sib]
    for k in range(1, TP):
        other = lax.rem(t + k, TP)
        greet.append((r, other))
        greet.append((rep(y, zh, 1 - c), other))
    for dev in greet:
        pl.semaphore_signal(barrier, inc=1, device_id=dev, device_id_type=MESH)
    pl.semaphore_wait(barrier, len(greet))

    load_x = [
        pltpu.make_async_copy(
            x_hbm.at[s, pl.ds(h * SIDE, SIDE)], xin.at[pl.ds(h * PART + s * SIDE, SIDE)], loc.at[4 + h * STEPS + s]
        )
        for h in range(PARTS)
        for s in range(STEPS)
    ]
    for copy in load_x:
        copy.start()
    kv = {}

    def load_kv(layer):
        kv[layer] = [
            pltpu.make_async_copy(k_hbm.at[layer], kbuf, loc.at[1]),
            pltpu.make_async_copy(v_hbm.at[layer], vbuf, loc.at[2]),
        ]
        for copy in kv[layer]:
            copy.start()

    def qcols(other):
        return pl.ds(pl.multiple_of(other * GROUP, GROUP), GROUP)

    slab = first, second = pl.ds(0, PAD), pl.ds(2 * OWN - PAD, PAD)
    skip = (0, PAD - OWN)
    half_of_t = lax.div(t, 4)
    slot1 = lax.rem(t, 4) * 2 + c
    for k in range(1, TP):
        other = lax.rem(t + k, TP)
        send(qw.at[first, qcols(other)], land_q.at[0, t], a2a_s.at[0, k], a2a_r.at[0, t], (r, other))
    own0 = pltpu.make_async_copy(qw.at[first, qcols(t)], land_q.at[0, t], a2a_r.at[0, t])
    own0.start()
    load_kv(0)

    def start_exchange():
        for layer in range(LAYERS):
            theirs = pl.ds(pl.multiple_of((1 - c) * HALF, HALF), HALF)
            mine = pl.ds(pl.multiple_of(c * HALF, HALF), HALF)
            send(ow.at[slab[layer], theirs], land_o.at[layer, c], ex_s.at[layer], ex_r.at[layer, c], dev_sib)
            pltpu.make_async_copy(ow.at[slab[layer], mine], land_o.at[layer, c], ex_r.at[layer, 2]).start()

    def sibling_slab():
        return pltpu.make_async_remote_copy(
            src_ref=qw.at[second, qcols(t)], dst_ref=land_q.at[1, slot1], send_sem=a2a_s.at[1, 0],
            recv_sem=a2a_r.at[1, slot1], device_id=dev_sib, device_id_type=MESH,
        )

    def start_second():
        for k in range(1, TP):
            other = lax.rem(t + k, TP)
            send(
                qw.at[second, qcols(other)], land_q.at[1, slot1], a2a_s.at[1, k], a2a_r.at[1, slot1],
                (rep(y, zh, half_of_t), other),
            )

        @pl.when(half_of_t == c)
        def _():
            pltpu.make_async_copy(qw.at[second, qcols(t)], land_q.at[1, slot1], a2a_r.at[1, slot1]).start()

        @pl.when(half_of_t != c)
        def _():
            sibling_slab().start()

    def pack_q(layer):
        for slot in range(TP):
            got(land_q.at[layer, slot], a2a_r.at[layer, slot])
        for slot in range(TP):
            pack[slot * OWN : (slot + 1) * OWN, :] = land_q[layer, slot].astype(f32)[skip[layer] : skip[layer] + OWN]
        if layer == 0:
            wq[0, p, pl.ds(pl.multiple_of(c * 320, 320), 320), :] = pack[...].astype(bf16)
        else:
            for k in range(4):
                wq[1, 4 * c + k, pl.ds(pl.multiple_of(p * 80, 80), 80), :] = pack[k * 80 : (k + 1) * 80, :].astype(bf16)

    def pack_o(layer):
        pltpu.make_async_copy(ow.at[slab[layer], pl.ds(0, HALF)], land_o.at[layer, c], ex_r.at[layer, 2]).wait()
        got(land_o.at[layer, 1 - c], ex_r.at[layer, 1 - c])
        for cut in range(4):
            cols = slice(cut * 512, (cut + 1) * 512)
            both = jnp.concatenate(
                [land_o[layer, core, :, cols].astype(f32)[skip[layer] : skip[layer] + OWN] for core in range(2)], axis=0
            )
            wo[layer, c, pl.ds(pl.multiple_of(p * 80, 80), 80), cols] = both.astype(bf16)

    def qblk(layer, y_, zh_, core):
        if layer == 0:
            return wq.at[0, y_ * 2 + zh_, pl.ds(pl.multiple_of(core * 320, 320), 320), :]
        return wq.at[1, pl.ds(4 * core, 4), pl.ds(pl.multiple_of((y_ * 2 + zh_) * 80, 80), 80), :]

    ring_y = [y, yp, y2, ym]

    def zsel(e):
        return zh if e == 0 else 1 - zh

    def oblk(layer, y_, zh_, core, part=None):
        cols = slice(None) if part is None else pl.ds(part * 1024, 1024)
        return wo.at[layer, core, pl.ds(pl.multiple_of((y_ * 2 + zh_) * 80, 80), 80), cols]

    streams = {
        ("q", 0): (qblk, q_s, q_r, True),
        ("q", 1): (qblk, q_s, q_r, True),
        ("o", 0): (oblk, o_s, o_r, O_Z_FIRST[0]),
        ("o", 1): (oblk, o_s, o_r, O_Z_FIRST[1]),
    }

    def w_send(name, d, e, dev, idx, *part):
        blk, ss, rs, _ = streams[name]
        b = blk(name[1], ring_y[d], zsel(e), c, *part)
        send(b, b, ss.at[name[1], idx], rs.at[name[1], idx], dev)

    def w_got(name, d, e, idx, *part):
        blk, _, rs, _ = streams[name]
        got(blk(name[1], ring_y[d], zsel(e), c, *part), rs.at[name[1], idx])

    def w_sib(name, d, e):
        w_send(name, d, e, dev_sib, 8 + d * 2 + e)

    def w_pass(name, d):
        w_send(name, d, 0, dev_z, 4 + d)
        w_sib(name, d, 0)

    def w_step(step, name):
        if step == 5:
            blk, _, rs, _ = streams[name]
            for d in range(4):
                for e in range(2):
                    got(blk(name[1], ring_y[d], zsel(e), 1 - c), rs.at[name[1], 8 + d * 2 + e])
        elif streams[name][3]:
            if step == 1:
                w_send(name, 0, 0, dev_z, 0)
                w_send(name, 0, 0, dev_yp, 1)
                w_send(name, 0, 0, dev_ym, 3)
                w_sib(name, 0, 0)
            elif step == 2:
                w_got(name, 0, 1, 0)
                w_send(name, 0, 1, dev_yp, 2)
                w_send(name, 0, 1, dev_ym, 4)
                w_sib(name, 0, 1)
            elif step == 3:
                w_got(name, 3, 0, 1)
                w_send(name, 3, 0, dev_yp, 5)
                w_sib(name, 3, 0)
                w_got(name, 1, 0, 3)
                w_sib(name, 1, 0)
                w_got(name, 1, 1, 4)
                w_send(name, 1, 1, dev_ym, 6)
                w_sib(name, 1, 1)
                w_got(name, 3, 1, 2)
                w_sib(name, 3, 1)
            else:
                w_got(name, 2, 0, 5)
                w_sib(name, 2, 0)
                w_got(name, 2, 1, 6)
                w_sib(name, 2, 1)
        else:
            if step == 1:
                w_send(name, 0, 0, dev_yp, 0)
                w_send(name, 0, 0, dev_ym, 1)
                w_pass(name, 0)
            elif step == 2:
                w_got(name, 3, 0, 0)
                w_send(name, 3, 0, dev_yp, 2, 0)
                w_pass(name, 3)
                w_got(name, 1, 0, 1)
                w_send(name, 1, 0, dev_ym, 3, 1)
                w_pass(name, 1)
            elif step == 3:
                w_got(name, 2, 0, 2, 0)
                w_got(name, 2, 0, 3, 1)
                w_pass(name, 2)
            else:
                for d in (0, 3, 1, 2):
                    w_got(name, d, 1, 4 + d)
                    w_sib(name, d, 1)

    def q(step, layer):
        w_step(step, ("q", layer))

    def o(step, layer):
        w_step(step, ("o", layer))

    ring_x = [x, xp, lax.rem(x + 2, 4), xm]

    def tsel(d, e):
        return ring_x[d] * 2 + (zl if e == 0 else 1 - zl)

    def g_blk(n, d, e, part):
        b = refs[n](tsel(d, e))
        return b if part is None else b.at[pl.ds(part * (PART // 2), PART // 2)]

    def g_send(n, d, e, dev, idx, own=None, part=None):
        b = g_blk(n, d, e, part)
        send(b if own is None else own, b, g_s.at[n, idx], g_r.at[n, idx], dev)

    def g_got(n, d, e, idx, part=None):
        got(g_blk(n, d, e, part), g_r.at[n, idx])

    def g(step, n, own=None):
        if G_Z_FIRST[n]:
            if step == 1:
                g_send(n, 0, 0, dev_zl, 0, own)
                g_send(n, 0, 0, dev_xp, 1, own)
                g_send(n, 0, 0, dev_xm, 3, own)
            elif step == 2:
                g_got(n, 0, 1, 0)
                g_send(n, 0, 1, dev_xp, 2)
                g_send(n, 0, 1, dev_xm, 4)
            elif step == 3:
                g_got(n, 3, 0, 1)
                g_send(n, 3, 0, dev_xp, 5)
                g_got(n, 1, 0, 3)
                g_got(n, 1, 1, 4)
                g_send(n, 1, 1, dev_xm, 6)
                g_got(n, 3, 1, 2)
            else:
                g_got(n, 2, 0, 5)
                g_got(n, 2, 1, 6)
        else:
            if step == 1:
                g_send(n, 0, 0, dev_xp, 0, own)
                g_send(n, 0, 0, dev_xm, 1, own)
                g_send(n, 0, 0, dev_zl, 4, own)
            elif step == 2:
                g_got(n, 3, 0, 0)
                g_send(n, 3, 0, dev_xp, 2, part=0)
                g_send(n, 3, 0, dev_zl, 7)
                g_got(n, 1, 0, 1)
                g_send(n, 1, 0, dev_xm, 3, part=1)
                g_send(n, 1, 0, dev_zl, 5)
            elif step == 3:
                g_got(n, 2, 0, 2, 0)
                g_got(n, 2, 0, 3, 1)
                g_send(n, 2, 0, dev_zl, 6)
            else:
                for d in range(4):
                    g_got(n, d, 1, 4 + d)

    def prepare():
        diagonal = lax.broadcasted_iota(jnp.int32, (ROWS, ROWS), 0) == lax.broadcasted_iota(jnp.int32, (ROWS, ROWS), 1)
        length = jnp.sum(
            jnp.where(diagonal, jnp.broadcast_to(rows_len[...].astype(f32), (ROWS, ROWS)), 0.0), axis=1, keepdims=True
        )
        limit[...] = jnp.broadcast_to(length, (ROWS, SLOTS))
        flip = jnp.where(lax.broadcasted_iota(jnp.int32, (1, HEAD), 1) < HEAD // 2, -1.0, 1.0)
        for h in range(PARTS):
            for s in range(STEPS):
                angles = (length[h * SIDE : (h + 1) * SIDE] + float(s)) * frequency[...]
                rows = slice(h * PART + s * SIDE, h * PART + (s + 1) * SIDE)
                cosf[rows, :] = jnp.cos(angles)
                sinf[rows, :] = jnp.sin(angles) * flip
        for j in range(CHUNKS):
            gain[j : j + 1, :] = gains[0:1, j * CHUNK : (j + 1) * CHUNK]
            gain[CHUNKS + j : CHUNKS + j + 1, :] = jnp.concatenate(
                [gains[1:2, k * 320 + j * OWN : k * 320 + (j + 1) * OWN] for k in range(16)], axis=1
            )

    def pick_own():
        src = lax.broadcasted_iota(jnp.int32, (CHUNK, 256), 0)
        dst = lax.broadcasted_iota(jnp.int32, (CHUNK, 256), 1)
        for j in range(CHUNKS):
            base, shift = j * 80 // 128 * 128, j * 80 % 128
            place = dst - shift
            wanted = jnp.where(place < OWN, place + t * OWN, place + (320 - OWN) + t * OWN)
            ok = jnp.logical_and(jnp.logical_and(place >= 0, place < 2 * OWN), src == wanted)
            pick = jnp.where(ok, 1.0, 0.0).astype(bf16)
            mine = jnp.dot(xin[:, j * CHUNK : (j + 1) * CHUNK], pick, preferred_element_type=f32)
            width = min(256, CHUNK - base)
            if j == 0:
                resid[...] = jnp.zeros_like(resid)
            resid[:, base : base + width] += mine[:, :width]

    def normalize(layer, start, count, read):
        def body(b, carry):
            rows = pl.ds(pl.multiple_of(b * 32, 32), 32)
            inside = pl.ds(pl.multiple_of(b * 32 - start, 32), 32)
            total = jnp.zeros((32, 1), f32)
            for j in range(CHUNKS):
                wide = read(inside, j).astype(f32)
                total = total + jnp.sum(wide * wide, axis=-1, keepdims=True)
            scale = lax.rsqrt(total * (1.0 / D) + epsilon)
            for j in range(CHUNKS):
                norm[j, rows, :] = (read(inside, j).astype(f32) * scale * gain[layer * CHUNKS + j : layer * CHUNKS + j + 1, :]).astype(bf16)
            return carry

        lax.fori_loop(start // 32, (start + count) // 32, body, 0)

    def project_in(layer, start, count):
        rows = slice(start, start + count)
        mixed[rows, :] = jnp.zeros((count, GROUP), f32)

        def body(j, carry):
            mixed[rows, :] += jnp.dot(norm[j, rows], wq[layer, j], preferred_element_type=f32)
            return carry

        lax.fori_loop(0, CHUNKS, body, 0)

        def turn(v, g):
            n = v * lax.rsqrt(jnp.mean(v * v, axis=-1, keepdims=True) + epsilon) * g
            return n * cosf[rows, :] + pltpu.roll(n, HEAD // 2, 1) * sinf[rows, :]

        for i in range(4):
            turned = turn(mixed[rows, i * HEAD : (i + 1) * HEAD], qgain[layer])
            for h in range(start // PART, (start + count) // PART):
                for s in range(STEPS):
                    at = h * PART + s * SIDE - start
                    to = (s * 4 + i) * ROWS + h * SIDE
                    qs[to : to + SIDE, :] = turned[at : at + SIDE]
        nk[rows, :] = turn(mixed[rows, 4 * HEAD : 5 * HEAD], kgain[layer])
        nv[rows, :] = mixed[rows, 5 * HEAD : 6 * HEAD]

    row = lax.broadcasted_iota(jnp.int32, (128, 32), 0)
    col = lax.broadcasted_iota(jnp.int32, (128, 32), 1)
    fresh = jnp.logical_and(
        jnp.right_shift(row, 4) == jnp.bitwise_and(col, 7),
        jnp.right_shift(col, 3) <= jnp.bitwise_and(jnp.right_shift(row, 2), 3),
    )
    slot_index = lax.broadcasted_iota(jnp.int32, (16, SLOTS), 1).astype(f32)

    def attend(layer, h):
        if h == 0:
            for copy in kv[layer]:
                copy.wait()

        def body(b, carry):
            query = [qs[pl.ds(b * 8 + k, 16, stride=ROWS), :].astype(bf16) for k in range(8)]
            old = []
            for k in range(8):
                score = lax.dot_general(query[k], kbuf[b * 8 + k], NT, preferred_element_type=f32) * HEAD ** (-0.5)
                old.append(jnp.where(slot_index < limit[pl.ds(b * 8 + k, 1), :], score, -jnp.inf))
            old = jnp.concatenate(old, axis=0)
            part = [pl.ds(pl.multiple_of(h * (PART - SIDE) + s * SIDE + b * 8, 8), 8) for s in range(STEPS)]
            keys = jnp.concatenate([nk[w, :] for w in part], axis=0).astype(bf16)
            values = jnp.concatenate([nv[w, :] for w in part], axis=0).astype(bf16)
            new = lax.dot_general(jnp.concatenate(query, axis=0), keys, NT, preferred_element_type=f32) * HEAD ** (-0.5)
            new = jnp.where(fresh, new, -jnp.inf)
            top = jnp.maximum(jnp.max(old, axis=-1, keepdims=True), jnp.max(new, axis=-1, keepdims=True))
            old = jnp.exp(old - top)
            new = jnp.exp(new - top)
            below = jnp.sum(old, axis=-1, keepdims=True) + jnp.sum(new, axis=-1, keepdims=True)
            old = (old / below).astype(bf16)
            new = (new / below).astype(bf16)
            fresh_part = jnp.dot(new, values, preferred_element_type=f32)
            for k in range(8):
                rows = slice(k * 16, (k + 1) * 16)
                ao[pl.ds(b * 8 + k, 16, stride=ROWS), :] = (
                    jnp.dot(old[rows], vbuf[b * 8 + k], preferred_element_type=f32) + fresh_part[rows]
                )
            return carry

        lax.fori_loop(h * SIDE // 8, (h + 1) * SIDE // 8, body, 0)
        for s in range(STEPS):
            for i in range(4):
                start = (s * 4 + i) * ROWS + h * SIDE
                att[layer, h, t, s * SIDE : (s + 1) * SIDE, i * HEAD : (i + 1) * HEAD] = ao[
                    start : start + SIDE, :
                ].astype(bf16)

    def project_out(layer, h, before):
        total = jnp.zeros((PART, CHUNK), f32)
        for k in range(TP):
            total = total + lax.dot_general(
                att[layer, h, k], wo[layer, k // 4, :, (k % 4) * ATT : (k % 4 + 1) * ATT], NT,
                preferred_element_type=f32,
            )
        return (before.astype(f32) + total).astype(bf16)

    def att_ref(layer, h):
        return lambda k: att.at[layer, h, k]

    def hid_ref(h):
        return lambda k: hid.at[h, k]

    def out_ref(h):
        return lambda k: out.at[h, k]

    refs = [
        att_ref(0, 0), att_ref(0, 1), hid_ref(0), hid_ref(1), att_ref(1, 0), att_ref(1, 1), out_ref(0), out_ref(1)
    ]

    def first_out(h):
        hid[h, t] = project_out(0, h, resid[h * PART : (h + 1) * PART, :])
        g(1, 2 + h)

    def second_in(h):
        normalize(1, h * PART, PART, lambda rows, j: hid[h, j, rows, :])
        project_in(1, h * PART, PART)
        attend(1, h)
        g(1, 4 + h)

    keep = [pltpu.make_async_copy(hown.at[h], out.at[h, t], loc.at[3 * h]) for h in range(PARTS)]

    def second_out(h):
        hown[h] = project_out(1, h, hid[h, t])
        g(1, 6 + h, hown.at[h])
        keep[h].start()

    start_exchange()
    prepare()
    pack_o(0)
    pack_q(0)
    q(1,0)
    start_second()
    pack_o(1)
    for copy in load_x:
        copy.wait()
    pick_own()
    normalize(0, 0, FLAT, lambda rows, j: xin[rows, j * CHUNK : (j + 1) * CHUNK])
    q(2,0)
    q(3,0)
    pack_q(1)
    q(1,1)
    o(1,0)
    q(4,0)
    q(5,0)
    project_in(0,0,FLAT)
    attend(0,0)
    g(1,0)
    o(2,0)
    attend(0,1)
    g(1,1)
    load_kv(1)
    g(2,0)
    g(2,1)
    g(3,0)
    o(3,0)
    g(3,1)
    q(2,1)
    g(4,0)
    o(4,0)
    g(4,1)
    o(5,0)
    first_out(0)
    first_out(1)
    q(3,1)
    g(2,2)
    g(2,3)
    o(1,1)
    g(3,2)
    g(3,3)
    g(4,2)
    q(4,1)
    q(5,1)
    second_in(0)
    o(2,1)
    g(4,3)
    second_in(1)
    g(2,4)
    g(2,5)
    o(3,1)
    g(3,4)
    g(3,5)
    g(4,4)
    o(4,1)
    o(5,1)
    second_out(0)
    g(4,5)
    second_out(1)
    g(2,6)
    g(2,7)
    g(3,6)
    g(3,7)
    g(4,6)
    g(4,7)
    for copy in keep:
        copy.wait()
    for copy in sent:
        copy.wait_send()

    @pl.when(half_of_t != c)
    def _():
        sibling_slab().wait_send()


def fused(*operands):
    whole = pl.BlockSpec(memory_space=pltpu.VMEM)
    anywhere = pl.BlockSpec(memory_space=pl.ANY)
    dma = pltpu.SemaphoreType.DMA
    return pl.pallas_call(
        kernel,
        out_shape=jax.ShapeDtypeStruct((PARTS, TP, PART, CHUNK), bf16),
        in_specs=[anywhere] * 3 + [whole] * 5 + [anywhere] * 2,
        out_specs=anywhere,
        scratch_shapes=[
            pltpu.VMEM((LAYERS, CHUNKS, CHUNK, GROUP), bf16),
            pltpu.VMEM((LAYERS, 2, CHUNK, HALF), bf16),
            pltpu.VMEM((LAYERS, TP, PAD, GROUP), bf16),
            pltpu.VMEM((LAYERS, 2, PAD, HALF), bf16),
            pltpu.VMEM((TP * OWN, GROUP), f32),
            pltpu.VMEM((FLAT, D), bf16),
            pltpu.VMEM((CHUNKS, FLAT, CHUNK), bf16),
            pltpu.VMEM((PARTS, TP, PART, CHUNK), bf16),
            pltpu.VMEM((PARTS, PART, CHUNK), bf16),
            pltpu.VMEM((LAYERS, PARTS, TP, PART, ATT), bf16),
            pltpu.VMEM((ROWS, SLOTS, HEAD), bf16),
            pltpu.VMEM((ROWS, SLOTS, HEAD), bf16),
            pltpu.VMEM((16 * ROWS, HEAD), f32),
            pltpu.VMEM((16 * ROWS, HEAD), f32),
            pltpu.VMEM((FLAT, HEAD), f32),
            pltpu.VMEM((FLAT, HEAD), f32),
            pltpu.VMEM((FLAT, GROUP), f32),
            pltpu.VMEM((FLAT, CHUNK), f32),
            pltpu.VMEM((LAYERS * CHUNKS, CHUNK), f32),
            pltpu.VMEM((FLAT, HEAD), f32),
            pltpu.VMEM((FLAT, HEAD), f32),
            pltpu.VMEM((ROWS, SLOTS), f32),
            dma((LAYERS, TP)), dma((LAYERS, TP)),
            dma((LAYERS,)), dma((LAYERS, 3)),
            dma((LAYERS, 16)), dma((LAYERS, 16)),
            dma((LAYERS, 16)), dma((LAYERS, 16)),
            dma((4 * PARTS, 8)), dma((4 * PARTS, 8)),
            dma((4 + PARTS * STEPS,)),
        ],
        compiler_params=pltpu.CompilerParams(
            collective_id=0, has_side_effects=True, vmem_limit_bytes=60 * 1024 * 1024
        ),
    )(*operands)


def restore_kernel(hidden, natural):
    for p in range(CHUNKS):
        window = slice(p * 80 // 128 * 128, -(-(p + 1) * 80 // 128) * 128)
        wide = [hidden[0, k, :, window].astype(f32) for k in range(TP)]
        start = p * 80 % 128
        parts = [wide[k][:, start + core * OWN : start + (core + 1) * OWN] for core in range(2) for k in range(TP)]
        natural[0, :, p * CHUNK : (p + 1) * CHUNK] = jnp.concatenate(parts, axis=1).astype(bf16)


def restore(hidden):
    return pl.pallas_call(
        restore_kernel,
        out_shape=jax.ShapeDtypeStruct((STEPS, ROWS, D), bf16),
        grid=(PARTS, STEPS),
        in_specs=[pl.BlockSpec((1, TP, SIDE, CHUNK), lambda h, s: (h, 0, s, 0))],
        out_specs=pl.BlockSpec((1, SIDE, D), lambda h, s: (s, h, 0)),
        compiler_params=pltpu.CompilerParams(vmem_limit_bytes=32 * 1024 * 1024),
    )(hidden)


def on_device(
    inputs, qkv_weight, out_weight, norm_gain, query_gain, key_gain, stored_rotated_keys, stored_cache_values, lengths
):
    half = HEAD // 2
    frequency = rope_base ** (-jnp.arange(half, dtype=f32) / half)
    hidden = fused(
        inputs,
        qkv_weight.reshape(LAYERS * OWN, TP * GROUP),
        out_weight.reshape(LAYERS * OWN, TP * ATT),
        norm_gain,
        query_gain.reshape(LAYERS, 1, HEAD),
        key_gain.reshape(LAYERS, 1, HEAD),
        lengths.reshape(1, ROWS),
        jnp.concatenate([frequency, frequency]).reshape(1, HEAD),
        stored_rotated_keys.reshape(LAYERS, ROWS, SLOTS, HEAD),
        stored_cache_values.reshape(LAYERS, ROWS, SLOTS, HEAD),
    )
    return restore(hidden)


def solution(mesh):
    return jax.shard_map(
        on_device,
        mesh=mesh,
        in_specs=(
            P(None, "rep", None),
            P(None, ("rep", "tp"), None),
            P(None, ("rep", "tp"), None),
            P(),
            P(),
            P(),
            P(None, "rep", "tp", None, None),
            P(None, "rep", "tp", None, None),
            P("rep"),
        ),
        out_specs=P(None, "rep", None),
        check_vma=False,
    )
```

```python
import functools

import jax
import jax.numpy as jnp
from jax import lax
from jax.experimental import pallas as pl
from jax.experimental.pallas import tpu as pltpu
from jax.sharding import PartitionSpec as P

MESH = pl.DeviceIdType.MESH
epsilon = 1e-06
rope_base = 1000000.0

LAYERS = 2
STEPS = 4
ROWS = 64
FLAT = STEPS * ROWS
PARTS = 2
SIDE = ROWS // PARTS
PART = FLAT // PARTS
D = 5120
CHUNKS = 8
CHUNK = D // CHUNKS
OWN = 40
PAD = 48
HEAD = 128
GROUP = 768
ATT = 512
SLOTS = 256
HALF = 2048
TP = 8
f32 = jnp.float32
bf16 = jnp.bfloat16

O_Z_FIRST = (True, True)
G_Z_FIRST = (True, False, True, False, True, False, True, False)
NT = (((1,), (1,)), ((), ()))


def kernel(
    x_hbm, qw, ow, gains, qgain, kgain, rows_len, frequency, k_hbm, v_hbm,
    out,
    wq, wo, land_q, land_o, pack, xin, norm, hid, hown, att, kbuf, vbuf, qs, ao, nk, nv, mixed, resid, gain, cosf, sinf, limit,
    a2a_s, a2a_r, ex_s, ex_r, q_s, q_r, o_s, o_r, g_s, g_r, loc,
):
    r = lax.axis_index("rep")
    t = lax.axis_index("tp")
    y = lax.div(r, 4)
    zh = lax.rem(lax.div(r, 2), 2)
    c = lax.rem(r, 2)
    p = lax.div(r, 2)
    x = lax.div(t, 2)
    zl = lax.rem(t, 2)

    def rep(y_, zh_, c_):
        return y_ * 4 + zh_ * 2 + c_

    yp, ym, y2 = lax.rem(y + 1, 4), lax.rem(y + 3, 4), lax.rem(y + 2, 4)
    xp, xm = lax.rem(x + 1, 4), lax.rem(x + 3, 4)
    dev_yp = (rep(yp, zh, c), t)
    dev_ym = (rep(ym, zh, c), t)
    dev_z = (rep(y, 1 - zh, c), t)
    dev_sib = (rep(y, zh, 1 - c), t)
    dev_xp = (r, xp * 2 + zl)
    dev_xm = (r, xm * 2 + zl)
    dev_zl = (r, x * 2 + 1 - zl)

    sent = []

    def send(src, dst, ss, rs, dev):
        copy = pltpu.make_async_remote_copy(
            src_ref=src, dst_ref=dst, send_sem=ss, recv_sem=rs, device_id=dev, device_id_type=MESH
        )
        copy.start()
        sent.append(copy)

    def got(ref, rs):
        pltpu.make_async_remote_copy(
            src_ref=ref, dst_ref=ref, send_sem=rs, recv_sem=rs, device_id=dev_sib, device_id_type=MESH
        ).wait_recv()

    barrier = pltpu.get_barrier_semaphore()
    greet = [dev_yp, dev_ym, dev_z, dev_sib]
    for k in range(1, TP):
        other = lax.rem(t + k, TP)
        greet.append((r, other))
        greet.append((rep(y, zh, 1 - c), other))
    for dev in greet:
        pl.semaphore_signal(barrier, inc=1, device_id=dev, device_id_type=MESH)
    pl.semaphore_wait(barrier, len(greet))

    load_x = [
        pltpu.make_async_copy(
            x_hbm.at[s, pl.ds(h * SIDE, SIDE)], xin.at[pl.ds(h * PART + s * SIDE, SIDE)], loc.at[4 + h * STEPS + s]
        )
        for h in range(PARTS)
        for s in range(STEPS)
    ]
    for copy in load_x:
        copy.start()
    kv = {}

    def load_kv(layer):
        kv[layer] = [
            pltpu.make_async_copy(k_hbm.at[layer], kbuf, loc.at[1]),
            pltpu.make_async_copy(v_hbm.at[layer], vbuf, loc.at[2]),
        ]
        for copy in kv[layer]:
            copy.start()

    def qcols(other):
        return pl.ds(pl.multiple_of(other * GROUP, GROUP), GROUP)

    slab = first, second = pl.ds(0, PAD), pl.ds(2 * OWN - PAD, PAD)
    skip = (0, PAD - OWN)
    half_of_t = lax.div(t, 4)
    slot1 = lax.rem(t, 4) * 2 + c
    for k in range(1, TP):
        other = lax.rem(t + k, TP)
        send(qw.at[first, qcols(other)], land_q.at[0, t], a2a_s.at[0, k], a2a_r.at[0, t], (r, other))
    own0 = pltpu.make_async_copy(qw.at[first, qcols(t)], land_q.at[0, t], a2a_r.at[0, t])
    own0.start()
    load_kv(0)

    def start_exchange():
        for layer in range(LAYERS):
            theirs = pl.ds(pl.multiple_of((1 - c) * HALF, HALF), HALF)
            mine = pl.ds(pl.multiple_of(c * HALF, HALF), HALF)
            send(ow.at[slab[layer], theirs], land_o.at[layer, c], ex_s.at[layer], ex_r.at[layer, c], dev_sib)
            pltpu.make_async_copy(ow.at[slab[layer], mine], land_o.at[layer, c], ex_r.at[layer, 2]).start()

    def sibling_slab():
        return pltpu.make_async_remote_copy(
            src_ref=qw.at[second, qcols(t)], dst_ref=land_q.at[1, slot1], send_sem=a2a_s.at[1, 0],
            recv_sem=a2a_r.at[1, slot1], device_id=dev_sib, device_id_type=MESH,
        )

    def start_second():
        for k in range(1, TP):
            other = lax.rem(t + k, TP)
            send(
                qw.at[second, qcols(other)], land_q.at[1, slot1], a2a_s.at[1, k], a2a_r.at[1, slot1],
                (rep(y, zh, half_of_t), other),
            )

        @pl.when(half_of_t == c)
        def _():
            pltpu.make_async_copy(qw.at[second, qcols(t)], land_q.at[1, slot1], a2a_r.at[1, slot1]).start()

        @pl.when(half_of_t != c)
        def _():
            sibling_slab().start()

    def pack_q(layer):
        for slot in range(TP):
            got(land_q.at[layer, slot], a2a_r.at[layer, slot])
        for slot in range(TP):
            pack[slot * OWN : (slot + 1) * OWN, :] = land_q[layer, slot].astype(f32)[skip[layer] : skip[layer] + OWN]
        if layer == 0:
            wq[0, p, pl.ds(pl.multiple_of(c * 320, 320), 320), :] = pack[...].astype(bf16)
        else:
            for k in range(4):
                wq[1, 4 * c + k, pl.ds(pl.multiple_of(p * 80, 80), 80), :] = pack[k * 80 : (k + 1) * 80, :].astype(bf16)

    def pack_o(layer):
        pltpu.make_async_copy(ow.at[slab[layer], pl.ds(0, HALF)], land_o.at[layer, c], ex_r.at[layer, 2]).wait()
        got(land_o.at[layer, 1 - c], ex_r.at[layer, 1 - c])
        for cut in range(4):
            cols = slice(cut * 512, (cut + 1) * 512)
            both = jnp.concatenate(
                [land_o[layer, core, :, cols].astype(f32)[skip[layer] : skip[layer] + OWN] for core in range(2)], axis=0
            )
            wo[layer, c, pl.ds(pl.multiple_of(p * 80, 80), 80), cols] = both.astype(bf16)

    def qblk(layer, y_, zh_, core):
        if layer == 0:
            return wq.at[0, y_ * 2 + zh_, pl.ds(pl.multiple_of(core * 320, 320), 320), :]
        return wq.at[1, pl.ds(4 * core, 4), pl.ds(pl.multiple_of((y_ * 2 + zh_) * 80, 80), 80), :]

    ring_y = [y, yp, y2, ym]

    def zsel(e):
        return zh if e == 0 else 1 - zh

    def oblk(layer, y_, zh_, core, part=None):
        cols = slice(None) if part is None else pl.ds(part * 1024, 1024)
        return wo.at[layer, core, pl.ds(pl.multiple_of((y_ * 2 + zh_) * 80, 80), 80), cols]

    streams = {
        ("q", 0): (qblk, q_s, q_r, True),
        ("q", 1): (qblk, q_s, q_r, True),
        ("o", 0): (oblk, o_s, o_r, O_Z_FIRST[0]),
        ("o", 1): (oblk, o_s, o_r, O_Z_FIRST[1]),
    }

    def w_send(name, d, e, dev, idx, *part):
        blk, ss, rs, _ = streams[name]
        b = blk(name[1], ring_y[d], zsel(e), c, *part)
        send(b, b, ss.at[name[1], idx], rs.at[name[1], idx], dev)

    def w_got(name, d, e, idx, *part):
        blk, _, rs, _ = streams[name]
        got(blk(name[1], ring_y[d], zsel(e), c, *part), rs.at[name[1], idx])

    def w_sib(name, d, e):
        w_send(name, d, e, dev_sib, 8 + d * 2 + e)

    def w_pass(name, d):
        w_send(name, d, 0, dev_z, 4 + d)
        w_sib(name, d, 0)

    def w_step(step, name):
        if step == 5:
            blk, _, rs, _ = streams[name]
            for d in range(4):
                for e in range(2):
                    got(blk(name[1], ring_y[d], zsel(e), 1 - c), rs.at[name[1], 8 + d * 2 + e])
        elif streams[name][3]:
            if step == 1:
                w_send(name, 0, 0, dev_z, 0)
                w_send(name, 0, 0, dev_yp, 1)
                w_send(name, 0, 0, dev_ym, 3)
                w_sib(name, 0, 0)
            elif step == 2:
                w_got(name, 0, 1, 0)
                w_send(name, 0, 1, dev_yp, 2)
                w_send(name, 0, 1, dev_ym, 4)
                w_sib(name, 0, 1)
            elif step == 3:
                w_got(name, 3, 0, 1)
                w_send(name, 3, 0, dev_yp, 5)
                w_sib(name, 3, 0)
                w_got(name, 1, 0, 3)
                w_sib(name, 1, 0)
                w_got(name, 1, 1, 4)
                w_send(name, 1, 1, dev_ym, 6)
                w_sib(name, 1, 1)
                w_got(name, 3, 1, 2)
                w_sib(name, 3, 1)
            else:
                w_got(name, 2, 0, 5)
                w_sib(name, 2, 0)
                w_got(name, 2, 1, 6)
                w_sib(name, 2, 1)
        else:
            if step == 1:
                w_send(name, 0, 0, dev_yp, 0)
                w_send(name, 0, 0, dev_ym, 1)
                w_pass(name, 0)
            elif step == 2:
                w_got(name, 3, 0, 0)
                w_send(name, 3, 0, dev_yp, 2, 0)
                w_pass(name, 3)
                w_got(name, 1, 0, 1)
                w_send(name, 1, 0, dev_ym, 3, 1)
                w_pass(name, 1)
            elif step == 3:
                w_got(name, 2, 0, 2, 0)
                w_got(name, 2, 0, 3, 1)
                w_pass(name, 2)
            else:
                for d in (0, 3, 1, 2):
                    w_got(name, d, 1, 4 + d)
                    w_sib(name, d, 1)

    def q(step, layer):
        w_step(step, ("q", layer))

    def o(step, layer):
        w_step(step, ("o", layer))

    ring_x = [x, xp, lax.rem(x + 2, 4), xm]

    def tsel(d, e):
        return ring_x[d] * 2 + (zl if e == 0 else 1 - zl)

    def g_blk(n, d, e, part):
        b = refs[n](tsel(d, e))
        return b if part is None else b.at[pl.ds(part * (PART // 2), PART // 2)]

    def g_send(n, d, e, dev, idx, own=None, part=None):
        b = g_blk(n, d, e, part)
        send(b if own is None else own, b, g_s.at[n, idx], g_r.at[n, idx], dev)

    def g_got(n, d, e, idx, part=None):
        got(g_blk(n, d, e, part), g_r.at[n, idx])

    def g(step, n, own=None):
        if G_Z_FIRST[n]:
            if step == 1:
                g_send(n, 0, 0, dev_zl, 0, own)
                g_send(n, 0, 0, dev_xp, 1, own)
                g_send(n, 0, 0, dev_xm, 3, own)
            elif step == 2:
                g_got(n, 0, 1, 0)
                g_send(n, 0, 1, dev_xp, 2)
                g_send(n, 0, 1, dev_xm, 4)
            elif step == 3:
                g_got(n, 3, 0, 1)
                g_send(n, 3, 0, dev_xp, 5)
                g_got(n, 1, 0, 3)
                g_got(n, 1, 1, 4)
                g_send(n, 1, 1, dev_xm, 6)
                g_got(n, 3, 1, 2)
            else:
                g_got(n, 2, 0, 5)
                g_got(n, 2, 1, 6)
        else:
            if step == 1:
                g_send(n, 0, 0, dev_xp, 0, own)
                g_send(n, 0, 0, dev_xm, 1, own)
                g_send(n, 0, 0, dev_zl, 4, own)
            elif step == 2:
                g_got(n, 3, 0, 0)
                g_send(n, 3, 0, dev_xp, 2, part=0)
                g_send(n, 3, 0, dev_zl, 7)
                g_got(n, 1, 0, 1)
                g_send(n, 1, 0, dev_xm, 3, part=1)
                g_send(n, 1, 0, dev_zl, 5)
            elif step == 3:
                g_got(n, 2, 0, 2, 0)
                g_got(n, 2, 0, 3, 1)
                g_send(n, 2, 0, dev_zl, 6)
            else:
                for d in range(4):
                    g_got(n, d, 1, 4 + d)

    def prepare():
        diagonal = lax.broadcasted_iota(jnp.int32, (ROWS, ROWS), 0) == lax.broadcasted_iota(jnp.int32, (ROWS, ROWS), 1)
        length = jnp.sum(
            jnp.where(diagonal, jnp.broadcast_to(rows_len[...].astype(f32), (ROWS, ROWS)), 0.0), axis=1, keepdims=True
        )
        limit[...] = jnp.broadcast_to(length, (ROWS, SLOTS))
        flip = jnp.where(lax.broadcasted_iota(jnp.int32, (1, HEAD), 1) < HEAD // 2, -1.0, 1.0)
        for h in range(PARTS):
            for s in range(STEPS):
                angles = (length[h * SIDE : (h + 1) * SIDE] + float(s)) * frequency[...]
                rows = slice(h * PART + s * SIDE, h * PART + (s + 1) * SIDE)
                cosf[rows, :] = jnp.cos(angles)
                sinf[rows, :] = jnp.sin(angles) * flip
        for j in range(CHUNKS):
            gain[j : j + 1, :] = gains[0:1, j * CHUNK : (j + 1) * CHUNK]
            gain[CHUNKS + j : CHUNKS + j + 1, :] = jnp.concatenate(
                [gains[1:2, k * 320 + j * OWN : k * 320 + (j + 1) * OWN] for k in range(16)], axis=1
            )

    def pick_own():
        src = lax.broadcasted_iota(jnp.int32, (CHUNK, 256), 0)
        dst = lax.broadcasted_iota(jnp.int32, (CHUNK, 256), 1)
        for j in range(CHUNKS):
            base, shift = j * 80 // 128 * 128, j * 80 % 128
            place = dst - shift
            wanted = jnp.where(place < OWN, place + t * OWN, place + (320 - OWN) + t * OWN)
            ok = jnp.logical_and(jnp.logical_and(place >= 0, place < 2 * OWN), src == wanted)
            pick = jnp.where(ok, 1.0, 0.0).astype(bf16)
            mine = jnp.dot(xin[:, j * CHUNK : (j + 1) * CHUNK], pick, preferred_element_type=f32)
            width = min(256, CHUNK - base)
            if j == 0:
                resid[...] = jnp.zeros_like(resid)
            resid[:, base : base + width] += mine[:, :width]

    def normalize(layer, start, count, read):
        def body(b, carry):
            rows = pl.ds(pl.multiple_of(b * 32, 32), 32)
            inside = pl.ds(pl.multiple_of(b * 32 - start, 32), 32)
            total = jnp.zeros((32, 1), f32)
            for j in range(CHUNKS):
                wide = read(inside, j).astype(f32)
                total = total + jnp.sum(wide * wide, axis=-1, keepdims=True)
            scale = lax.rsqrt(total * (1.0 / D) + epsilon)
            for j in range(CHUNKS):
                norm[j, rows, :] = (read(inside, j).astype(f32) * scale * gain[layer * CHUNKS + j : layer * CHUNKS + j + 1, :]).astype(bf16)
            return carry

        lax.fori_loop(start // 32, (start + count) // 32, body, 0)

    def project_in(layer, start, count):
        rows = slice(start, start + count)
        mixed[rows, :] = jnp.zeros((count, GROUP), f32)

        def body(j, carry):
            mixed[rows, :] += jnp.dot(norm[j, rows], wq[layer, j], preferred_element_type=f32)
            return carry

        lax.fori_loop(0, CHUNKS, body, 0)

        def turn(v, g):
            n = v * lax.rsqrt(jnp.mean(v * v, axis=-1, keepdims=True) + epsilon) * g
            return n * cosf[rows, :] + pltpu.roll(n, HEAD // 2, 1) * sinf[rows, :]

        for i in range(4):
            turned = turn(mixed[rows, i * HEAD : (i + 1) * HEAD], qgain[layer])
            for h in range(start // PART, (start + count) // PART):
                for s in range(STEPS):
                    at = h * PART + s * SIDE - start
                    to = (s * 4 + i) * ROWS + h * SIDE
                    qs[to : to + SIDE, :] = turned[at : at + SIDE]
        nk[rows, :] = turn(mixed[rows, 4 * HEAD : 5 * HEAD], kgain[layer])
        nv[rows, :] = mixed[rows, 5 * HEAD : 6 * HEAD]

    row = lax.broadcasted_iota(jnp.int32, (128, 32), 0)
    col = lax.broadcasted_iota(jnp.int32, (128, 32), 1)
    fresh = jnp.logical_and(
        jnp.right_shift(row, 4) == jnp.bitwise_and(col, 7),
        jnp.right_shift(col, 3) <= jnp.bitwise_and(jnp.right_shift(row, 2), 3),
    )
    slot_index = lax.broadcasted_iota(jnp.int32, (16, SLOTS), 1).astype(f32)

    def attend(layer, h):
        if h == 0:
            for copy in kv[layer]:
                copy.wait()

        def body(b, carry):
            query = [qs[pl.ds(b * 8 + k, 16, stride=ROWS), :].astype(bf16) for k in range(8)]
            old = []
            for k in range(8):
                score = lax.dot_general(query[k], kbuf[b * 8 + k], NT, preferred_element_type=f32) * HEAD ** (-0.5)
                old.append(jnp.where(slot_index < limit[pl.ds(b * 8 + k, 1), :], score, -jnp.inf))
            old = jnp.concatenate(old, axis=0)
            part = [pl.ds(pl.multiple_of(h * (PART - SIDE) + s * SIDE + b * 8, 8), 8) for s in range(STEPS)]
            keys = jnp.concatenate([nk[w, :] for w in part], axis=0).astype(bf16)
            values = jnp.concatenate([nv[w, :] for w in part], axis=0).astype(bf16)
            new = lax.dot_general(jnp.concatenate(query, axis=0), keys, NT, preferred_element_type=f32) * HEAD ** (-0.5)
            new = jnp.where(fresh, new, -jnp.inf)
            top = jnp.maximum(jnp.max(old, axis=-1, keepdims=True), jnp.max(new, axis=-1, keepdims=True))
            old = jnp.exp(old - top)
            new = jnp.exp(new - top)
            below = jnp.sum(old, axis=-1, keepdims=True) + jnp.sum(new, axis=-1, keepdims=True)
            old = (old / below).astype(bf16)
            new = (new / below).astype(bf16)
            fresh_part = jnp.dot(new, values, preferred_element_type=f32)
            for k in range(8):
                rows = slice(k * 16, (k + 1) * 16)
                ao[pl.ds(b * 8 + k, 16, stride=ROWS), :] = (
                    jnp.dot(old[rows], vbuf[b * 8 + k], preferred_element_type=f32) + fresh_part[rows]
                )
            return carry

        lax.fori_loop(h * SIDE // 8, (h + 1) * SIDE // 8, body, 0)
        for s in range(STEPS):
            for i in range(4):
                start = (s * 4 + i) * ROWS + h * SIDE
                att[layer, h, t, s * SIDE : (s + 1) * SIDE, i * HEAD : (i + 1) * HEAD] = ao[
                    start : start + SIDE, :
                ].astype(bf16)

    def project_out(layer, h, before):
        total = jnp.zeros((PART, CHUNK), f32)
        for k in range(TP):
            total = total + lax.dot_general(
                att[layer, h, k], wo[layer, k // 4, :, (k % 4) * ATT : (k % 4 + 1) * ATT], NT,
                preferred_element_type=f32,
            )
        return (before.astype(f32) + total).astype(bf16)

    def att_ref(layer, h):
        return lambda k: att.at[layer, h, k]

    def hid_ref(h):
        return lambda k: hid.at[h, k]

    def out_ref(h):
        return lambda k: out.at[h, k]

    refs = [
        att_ref(0, 0), att_ref(0, 1), hid_ref(0), hid_ref(1), att_ref(1, 0), att_ref(1, 1), out_ref(0), out_ref(1)
    ]

    def first_out(h):
        hid[h, t] = project_out(0, h, resid[h * PART : (h + 1) * PART, :])
        g(1, 2 + h)

    def second_in(h):
        normalize(1, h * PART, PART, lambda rows, j: hid[h, j, rows, :])
        project_in(1, h * PART, PART)
        attend(1, h)
        g(1, 4 + h)

    keep = [pltpu.make_async_copy(hown.at[h], out.at[h, t], loc.at[3 * h]) for h in range(PARTS)]

    def second_out(h):
        hown[h] = project_out(1, h, hid[h, t])
        g(1, 6 + h, hown.at[h])
        keep[h].start()

    start_exchange()
    prepare()
    pack_o(0)
    pack_q(0)
    q(1,0)
    pack_o(1)
    for copy in load_x:
        copy.wait()
    normalize(0, 0, FLAT, lambda rows, j: xin[rows, j * CHUNK : (j + 1) * CHUNK])
    q(2,0)
    start_second()
    pick_own()
    q(3,0)
    pack_q(1)
    q(1,1)
    o(1,0)
    q(4,0)
    q(5,0)
    project_in(0,0,FLAT)
    attend(0,0)
    g(1,0)
    o(2,0)
    attend(0,1)
    g(1,1)
    load_kv(1)
    g(2,0)
    g(2,1)
    g(3,0)
    o(3,0)
    g(3,1)
    q(2,1)
    g(4,0)
    o(4,0)
    g(4,1)
    o(5,0)
    first_out(0)
    first_out(1)
    q(3,1)
    o(1,1)
    g(2,2)
    g(2,3)
    g(3,2)
    g(3,3)
    g(4,2)
    q(4,1)
    q(5,1)
    second_in(0)
    o(2,1)
    g(4,3)
    second_in(1)
    g(2,4)
    g(2,5)
    o(3,1)
    g(3,4)
    g(3,5)
    g(4,4)
    o(4,1)
    o(5,1)
    second_out(0)
    g(4,5)
    second_out(1)
    g(2,6)
    g(2,7)
    g(3,6)
    g(3,7)
    g(4,6)
    g(4,7)
    for copy in keep:
        copy.wait()
    for copy in sent:
        copy.wait_send()

    @pl.when(half_of_t != c)
    def _():
        sibling_slab().wait_send()


def fused(*operands):
    whole = pl.BlockSpec(memory_space=pltpu.VMEM)
    anywhere = pl.BlockSpec(memory_space=pl.ANY)
    dma = pltpu.SemaphoreType.DMA
    return pl.pallas_call(
        kernel,
        out_shape=jax.ShapeDtypeStruct((PARTS, TP, PART, CHUNK), bf16),
        in_specs=[anywhere] * 3 + [whole] * 5 + [anywhere] * 2,
        out_specs=anywhere,
        scratch_shapes=[
            pltpu.VMEM((LAYERS, CHUNKS, CHUNK, GROUP), bf16),
            pltpu.VMEM((LAYERS, 2, CHUNK, HALF), bf16),
            pltpu.VMEM((LAYERS, TP, PAD, GROUP), bf16),
            pltpu.VMEM((LAYERS, 2, PAD, HALF), bf16),
            pltpu.VMEM((TP * OWN, GROUP), f32),
            pltpu.VMEM((FLAT, D), bf16),
            pltpu.VMEM((CHUNKS, FLAT, CHUNK), bf16),
            pltpu.VMEM((PARTS, TP, PART, CHUNK), bf16),
            pltpu.VMEM((PARTS, PART, CHUNK), bf16),
            pltpu.VMEM((LAYERS, PARTS, TP, PART, ATT), bf16),
            pltpu.VMEM((ROWS, SLOTS, HEAD), bf16),
            pltpu.VMEM((ROWS, SLOTS, HEAD), bf16),
            pltpu.VMEM((16 * ROWS, HEAD), f32),
            pltpu.VMEM((16 * ROWS, HEAD), f32),
            pltpu.VMEM((FLAT, HEAD), f32),
            pltpu.VMEM((FLAT, HEAD), f32),
            pltpu.VMEM((FLAT, GROUP), f32),
            pltpu.VMEM((FLAT, CHUNK), f32),
            pltpu.VMEM((LAYERS * CHUNKS, CHUNK), f32),
            pltpu.VMEM((FLAT, HEAD), f32),
            pltpu.VMEM((FLAT, HEAD), f32),
            pltpu.VMEM((ROWS, SLOTS), f32),
            dma((LAYERS, TP)), dma((LAYERS, TP)),
            dma((LAYERS,)), dma((LAYERS, 3)),
            dma((LAYERS, 16)), dma((LAYERS, 16)),
            dma((LAYERS, 16)), dma((LAYERS, 16)),
            dma((4 * PARTS, 8)), dma((4 * PARTS, 8)),
            dma((4 + PARTS * STEPS,)),
        ],
        compiler_params=pltpu.CompilerParams(
            collective_id=0, has_side_effects=True, vmem_limit_bytes=60 * 1024 * 1024
        ),
    )(*operands)


def restore_kernel(hidden, natural):
    for p in range(CHUNKS):
        window = slice(p * 80 // 128 * 128, -(-(p + 1) * 80 // 128) * 128)
        wide = [hidden[0, k, :, window].astype(f32) for k in range(TP)]
        start = p * 80 % 128
        parts = [wide[k][:, start + core * OWN : start + (core + 1) * OWN] for core in range(2) for k in range(TP)]
        natural[0, :, p * CHUNK : (p + 1) * CHUNK] = jnp.concatenate(parts, axis=1).astype(bf16)


def restore(hidden):
    return pl.pallas_call(
        restore_kernel,
        out_shape=jax.ShapeDtypeStruct((STEPS, ROWS, D), bf16),
        grid=(PARTS, STEPS),
        in_specs=[pl.BlockSpec((1, TP, SIDE, CHUNK), lambda h, s: (h, 0, s, 0))],
        out_specs=pl.BlockSpec((1, SIDE, D), lambda h, s: (s, h, 0)),
        compiler_params=pltpu.CompilerParams(vmem_limit_bytes=32 * 1024 * 1024),
    )(hidden)


def on_device(
    inputs, qkv_weight, out_weight, norm_gain, query_gain, key_gain, stored_rotated_keys, stored_cache_values, lengths
):
    half = HEAD // 2
    frequency = rope_base ** (-jnp.arange(half, dtype=f32) / half)
    hidden = fused(
        inputs,
        qkv_weight.reshape(LAYERS * OWN, TP * GROUP),
        out_weight.reshape(LAYERS * OWN, TP * ATT),
        norm_gain,
        query_gain.reshape(LAYERS, 1, HEAD),
        key_gain.reshape(LAYERS, 1, HEAD),
        lengths.reshape(1, ROWS),
        jnp.concatenate([frequency, frequency]).reshape(1, HEAD),
        stored_rotated_keys.reshape(LAYERS, ROWS, SLOTS, HEAD),
        stored_cache_values.reshape(LAYERS, ROWS, SLOTS, HEAD),
    )
    return restore(hidden)


def solution(mesh):
    return jax.shard_map(
        on_device,
        mesh=mesh,
        in_specs=(
            P(None, "rep", None),
            P(None, ("rep", "tp"), None),
            P(None, ("rep", "tp"), None),
            P(),
            P(),
            P(),
            P(None, "rep", "tp", None, None),
            P(None, "rep", "tp", None, None),
            P("rep"),
        ),
        out_specs=P(None, "rep", None),
        check_vma=False,
    )
```

```python
import functools

import jax
import jax.numpy as jnp
from jax import lax
from jax.experimental import pallas as pl
from jax.experimental.pallas import tpu as pltpu
from jax.sharding import PartitionSpec as P

MESH = pl.DeviceIdType.MESH
epsilon = 1e-06
rope_base = 1000000.0

LAYERS = 2
STEPS = 4
ROWS = 64
FLAT = STEPS * ROWS
PARTS = 2
SIDE = ROWS // PARTS
PART = FLAT // PARTS
D = 5120
CHUNKS = 8
CHUNK = D // CHUNKS
OWN = 40
PAD = 48
HEAD = 128
GROUP = 768
ATT = 512
SLOTS = 256
HALF = 2048
TP = 8
f32 = jnp.float32
bf16 = jnp.bfloat16

O_Z_FIRST = (True, True)
G_Z_FIRST = (True, False, True, False, True, False, False, True)
NT = (((1,), (1,)), ((), ()))


def kernel(
    x_hbm, qw, ow, gains, qgain, kgain, rows_len, frequency, k_hbm, v_hbm,
    out,
    wq, wo, land_q, land_o, pack, xin, norm, hid, hown, att, kbuf, vbuf, qs, ao, nk, nv, mixed, resid, gain, cosf, sinf, limit,
    a2a_s, a2a_r, ex_s, ex_r, q_s, q_r, o_s, o_r, g_s, g_r, loc,
):
    r = lax.axis_index("rep")
    t = lax.axis_index("tp")
    y = lax.div(r, 4)
    zh = lax.rem(lax.div(r, 2), 2)
    c = lax.rem(r, 2)
    p = lax.div(r, 2)
    x = lax.div(t, 2)
    zl = lax.rem(t, 2)

    def rep(y_, zh_, c_):
        return y_ * 4 + zh_ * 2 + c_

    yp, ym, y2 = lax.rem(y + 1, 4), lax.rem(y + 3, 4), lax.rem(y + 2, 4)
    xp, xm = lax.rem(x + 1, 4), lax.rem(x + 3, 4)
    dev_yp = (rep(yp, zh, c), t)
    dev_ym = (rep(ym, zh, c), t)
    dev_z = (rep(y, 1 - zh, c), t)
    dev_sib = (rep(y, zh, 1 - c), t)
    dev_xp = (r, xp * 2 + zl)
    dev_xm = (r, xm * 2 + zl)
    dev_zl = (r, x * 2 + 1 - zl)

    sent = []

    def send(src, dst, ss, rs, dev):
        copy = pltpu.make_async_remote_copy(
            src_ref=src, dst_ref=dst, send_sem=ss, recv_sem=rs, device_id=dev, device_id_type=MESH
        )
        copy.start()
        sent.append(copy)

    def got(ref, rs):
        pltpu.make_async_remote_copy(
            src_ref=ref, dst_ref=ref, send_sem=rs, recv_sem=rs, device_id=dev_sib, device_id_type=MESH
        ).wait_recv()

    barrier = pltpu.get_barrier_semaphore()
    greet = [dev_yp, dev_ym, dev_z, dev_sib]
    for k in range(1, TP):
        other = lax.rem(t + k, TP)
        greet.append((r, other))
        greet.append((rep(y, zh, 1 - c), other))
    for dev in greet:
        pl.semaphore_signal(barrier, inc=1, device_id=dev, device_id_type=MESH)
    pl.semaphore_wait(barrier, len(greet))

    load_x = [
        pltpu.make_async_copy(
            x_hbm.at[s, pl.ds(h * SIDE, SIDE)], xin.at[pl.ds(h * PART + s * SIDE, SIDE)], loc.at[4 + h * STEPS + s]
        )
        for h in range(PARTS)
        for s in range(STEPS)
    ]
    for copy in load_x:
        copy.start()
    kv = {}

    def load_kv(layer):
        kv[layer] = [
            pltpu.make_async_copy(k_hbm.at[layer], kbuf, loc.at[1]),
            pltpu.make_async_copy(v_hbm.at[layer], vbuf, loc.at[2]),
        ]
        for copy in kv[layer]:
            copy.start()

    def qcols(other):
        return pl.ds(pl.multiple_of(other * GROUP, GROUP), GROUP)

    slab = first, second = pl.ds(0, PAD), pl.ds(2 * OWN - PAD, PAD)
    skip = (0, PAD - OWN)
    half_of_t = lax.div(t, 4)
    slot1 = lax.rem(t, 4) * 2 + c
    for k in range(1, TP):
        other = lax.rem(t + k, TP)
        send(qw.at[first, qcols(other)], land_q.at[0, t], a2a_s.at[0, k], a2a_r.at[0, t], (r, other))
    own0 = pltpu.make_async_copy(qw.at[first, qcols(t)], land_q.at[0, t], a2a_r.at[0, t])
    own0.start()
    load_kv(0)

    def start_exchange():
        for layer in range(LAYERS):
            theirs = pl.ds(pl.multiple_of((1 - c) * HALF, HALF), HALF)
            mine = pl.ds(pl.multiple_of(c * HALF, HALF), HALF)
            send(ow.at[slab[layer], theirs], land_o.at[layer, c], ex_s.at[layer], ex_r.at[layer, c], dev_sib)
            pltpu.make_async_copy(ow.at[slab[layer], mine], land_o.at[layer, c], ex_r.at[layer, 2]).start()

    def sibling_slab():
        return pltpu.make_async_remote_copy(
            src_ref=qw.at[second, qcols(t)], dst_ref=land_q.at[1, slot1], send_sem=a2a_s.at[1, 0],
            recv_sem=a2a_r.at[1, slot1], device_id=dev_sib, device_id_type=MESH,
        )

    def start_second():
        for k in range(1, TP):
            other = lax.rem(t + k, TP)
            send(
                qw.at[second, qcols(other)], land_q.at[1, slot1], a2a_s.at[1, k], a2a_r.at[1, slot1],
                (rep(y, zh, half_of_t), other),
            )

        @pl.when(half_of_t == c)
        def _():
            pltpu.make_async_copy(qw.at[second, qcols(t)], land_q.at[1, slot1], a2a_r.at[1, slot1]).start()

        @pl.when(half_of_t != c)
        def _():
            sibling_slab().start()

    def pack_q(layer):
        for slot in range(TP):
            got(land_q.at[layer, slot], a2a_r.at[layer, slot])
        for slot in range(TP):
            pack[slot * OWN : (slot + 1) * OWN, :] = land_q[layer, slot].astype(f32)[skip[layer] : skip[layer] + OWN]
        if layer == 0:
            wq[0, p, pl.ds(pl.multiple_of(c * 320, 320), 320), :] = pack[...].astype(bf16)
        else:
            for k in range(4):
                wq[1, 4 * c + k, pl.ds(pl.multiple_of(p * 80, 80), 80), :] = pack[k * 80 : (k + 1) * 80, :].astype(bf16)

    def pack_o(layer):
        pltpu.make_async_copy(ow.at[slab[layer], pl.ds(0, HALF)], land_o.at[layer, c], ex_r.at[layer, 2]).wait()
        got(land_o.at[layer, 1 - c], ex_r.at[layer, 1 - c])
        for cut in range(4):
            cols = slice(cut * 512, (cut + 1) * 512)
            both = jnp.concatenate(
                [land_o[layer, core, :, cols].astype(f32)[skip[layer] : skip[layer] + OWN] for core in range(2)], axis=0
            )
            wo[layer, c, pl.ds(pl.multiple_of(p * 80, 80), 80), cols] = both.astype(bf16)

    def qblk(layer, y_, zh_, core):
        if layer == 0:
            return wq.at[0, y_ * 2 + zh_, pl.ds(pl.multiple_of(core * 320, 320), 320), :]
        return wq.at[1, pl.ds(4 * core, 4), pl.ds(pl.multiple_of((y_ * 2 + zh_) * 80, 80), 80), :]

    ring_y = [y, yp, y2, ym]

    def zsel(e):
        return zh if e == 0 else 1 - zh

    def oblk(layer, y_, zh_, core, part=None):
        cols = slice(None) if part is None else pl.ds(part * 1024, 1024)
        return wo.at[layer, core, pl.ds(pl.multiple_of((y_ * 2 + zh_) * 80, 80), 80), cols]

    streams = {
        ("q", 0): (qblk, q_s, q_r, True),
        ("q", 1): (qblk, q_s, q_r, True),
        ("o", 0): (oblk, o_s, o_r, O_Z_FIRST[0]),
        ("o", 1): (oblk, o_s, o_r, O_Z_FIRST[1]),
    }

    def w_send(name, d, e, dev, idx, *part):
        blk, ss, rs, _ = streams[name]
        b = blk(name[1], ring_y[d], zsel(e), c, *part)
        send(b, b, ss.at[name[1], idx], rs.at[name[1], idx], dev)

    def w_got(name, d, e, idx, *part):
        blk, _, rs, _ = streams[name]
        got(blk(name[1], ring_y[d], zsel(e), c, *part), rs.at[name[1], idx])

    def w_sib(name, d, e):
        w_send(name, d, e, dev_sib, 8 + d * 2 + e)

    def w_pass(name, d):
        w_send(name, d, 0, dev_z, 4 + d)
        w_sib(name, d, 0)

    def w_step(step, name):
        if step == 5:
            blk, _, rs, _ = streams[name]
            for d in range(4):
                for e in range(2):
                    got(blk(name[1], ring_y[d], zsel(e), 1 - c), rs.at[name[1], 8 + d * 2 + e])
        elif streams[name][3]:
            if step == 1:
                w_send(name, 0, 0, dev_z, 0)
                w_send(name, 0, 0, dev_yp, 1)
                w_send(name, 0, 0, dev_ym, 3)
                w_sib(name, 0, 0)
            elif step == 2:
                w_got(name, 0, 1, 0)
                w_send(name, 0, 1, dev_yp, 2)
                w_send(name, 0, 1, dev_ym, 4)
                w_sib(name, 0, 1)
            elif step == 3:
                w_got(name, 3, 0, 1)
                w_send(name, 3, 0, dev_yp, 5)
                w_sib(name, 3, 0)
                w_got(name, 1, 0, 3)
                w_sib(name, 1, 0)
                w_got(name, 1, 1, 4)
                w_send(name, 1, 1, dev_ym, 6)
                w_sib(name, 1, 1)
                w_got(name, 3, 1, 2)
                w_sib(name, 3, 1)
            else:
                w_got(name, 2, 0, 5)
                w_sib(name, 2, 0)
                w_got(name, 2, 1, 6)
                w_sib(name, 2, 1)
        else:
            if step == 1:
                w_send(name, 0, 0, dev_yp, 0)
                w_send(name, 0, 0, dev_ym, 1)
                w_pass(name, 0)
            elif step == 2:
                w_got(name, 3, 0, 0)
                w_send(name, 3, 0, dev_yp, 2, 0)
                w_pass(name, 3)
                w_got(name, 1, 0, 1)
                w_send(name, 1, 0, dev_ym, 3, 1)
                w_pass(name, 1)
            elif step == 3:
                w_got(name, 2, 0, 2, 0)
                w_got(name, 2, 0, 3, 1)
                w_pass(name, 2)
            else:
                for d in (0, 3, 1, 2):
                    w_got(name, d, 1, 4 + d)
                    w_sib(name, d, 1)

    def q(step, layer):
        w_step(step, ("q", layer))

    def o(step, layer):
        w_step(step, ("o", layer))

    ring_x = [x, xp, lax.rem(x + 2, 4), xm]

    def tsel(d, e):
        return ring_x[d] * 2 + (zl if e == 0 else 1 - zl)

    def g_blk(n, d, e, part):
        b = refs[n](tsel(d, e))
        return b if part is None else b.at[pl.ds(part * (PART // 2), PART // 2)]

    def g_send(n, d, e, dev, idx, own=None, part=None):
        b = g_blk(n, d, e, part)
        send(b if own is None else own, b, g_s.at[n, idx], g_r.at[n, idx], dev)

    def g_got(n, d, e, idx, part=None):
        got(g_blk(n, d, e, part), g_r.at[n, idx])

    def g(step, n, own=None):
        if G_Z_FIRST[n]:
            if step == 1:
                g_send(n, 0, 0, dev_zl, 0, own)
                g_send(n, 0, 0, dev_xp, 1, own)
                g_send(n, 0, 0, dev_xm, 3, own)
            elif step == 2:
                g_got(n, 0, 1, 0)
                g_send(n, 0, 1, dev_xp, 2)
                g_send(n, 0, 1, dev_xm, 4)
            elif step == 3:
                g_got(n, 3, 0, 1)
                g_send(n, 3, 0, dev_xp, 5)
                g_got(n, 1, 0, 3)
                g_got(n, 1, 1, 4)
                g_send(n, 1, 1, dev_xm, 6)
                g_got(n, 3, 1, 2)
            else:
                g_got(n, 2, 0, 5)
                g_got(n, 2, 1, 6)
        else:
            if step == 1:
                g_send(n, 0, 0, dev_xp, 0, own)
                g_send(n, 0, 0, dev_xm, 1, own)
                g_send(n, 0, 0, dev_zl, 4, own)
            elif step == 2:
                g_got(n, 3, 0, 0)
                g_send(n, 3, 0, dev_xp, 2, part=0)
                g_send(n, 3, 0, dev_zl, 7)
                g_got(n, 1, 0, 1)
                g_send(n, 1, 0, dev_xm, 3, part=1)
                g_send(n, 1, 0, dev_zl, 5)
            elif step == 3:
                g_got(n, 2, 0, 2, 0)
                g_got(n, 2, 0, 3, 1)
                g_send(n, 2, 0, dev_zl, 6)
            else:
                for d in range(4):
                    g_got(n, d, 1, 4 + d)

    def prepare():
        diagonal = lax.broadcasted_iota(jnp.int32, (ROWS, ROWS), 0) == lax.broadcasted_iota(jnp.int32, (ROWS, ROWS), 1)
        length = jnp.sum(
            jnp.where(diagonal, jnp.broadcast_to(rows_len[...].astype(f32), (ROWS, ROWS)), 0.0), axis=1, keepdims=True
        )
        limit[...] = jnp.broadcast_to(length, (ROWS, SLOTS))
        flip = jnp.where(lax.broadcasted_iota(jnp.int32, (1, HEAD), 1) < HEAD // 2, -1.0, 1.0)
        for h in range(PARTS):
            for s in range(STEPS):
                angles = (length[h * SIDE : (h + 1) * SIDE] + float(s)) * frequency[...]
                rows = slice(h * PART + s * SIDE, h * PART + (s + 1) * SIDE)
                cosf[rows, :] = jnp.cos(angles)
                sinf[rows, :] = jnp.sin(angles) * flip
        for j in range(CHUNKS):
            gain[j : j + 1, :] = gains[0:1, j * CHUNK : (j + 1) * CHUNK]
            gain[CHUNKS + j : CHUNKS + j + 1, :] = jnp.concatenate(
                [gains[1:2, k * 320 + j * OWN : k * 320 + (j + 1) * OWN] for k in range(16)], axis=1
            )

    def pick_own():
        src = lax.broadcasted_iota(jnp.int32, (CHUNK, 256), 0)
        dst = lax.broadcasted_iota(jnp.int32, (CHUNK, 256), 1)
        for j in range(CHUNKS):
            base, shift = j * 80 // 128 * 128, j * 80 % 128
            place = dst - shift
            wanted = jnp.where(place < OWN, place + t * OWN, place + (320 - OWN) + t * OWN)
            ok = jnp.logical_and(jnp.logical_and(place >= 0, place < 2 * OWN), src == wanted)
            pick = jnp.where(ok, 1.0, 0.0).astype(bf16)
            mine = jnp.dot(xin[:, j * CHUNK : (j + 1) * CHUNK], pick, preferred_element_type=f32)
            width = min(256, CHUNK - base)
            if j == 0:
                resid[...] = jnp.zeros_like(resid)
            resid[:, base : base + width] += mine[:, :width]

    def normalize(layer, start, count, read):
        def body(b, carry):
            rows = pl.ds(pl.multiple_of(b * 32, 32), 32)
            inside = pl.ds(pl.multiple_of(b * 32 - start, 32), 32)
            total = jnp.zeros((32, 1), f32)
            for j in range(CHUNKS):
                wide = read(inside, j).astype(f32)
                total = total + jnp.sum(wide * wide, axis=-1, keepdims=True)
            scale = lax.rsqrt(total * (1.0 / D) + epsilon)
            for j in range(CHUNKS):
                norm[j, rows, :] = (read(inside, j).astype(f32) * scale * gain[layer * CHUNKS + j : layer * CHUNKS + j + 1, :]).astype(bf16)
            return carry

        lax.fori_loop(start // 32, (start + count) // 32, body, 0)

    def project_in(layer, start, count):
        rows = slice(start, start + count)
        mixed[rows, :] = jnp.zeros((count, GROUP), f32)

        def body(j, carry):
            mixed[rows, :] += jnp.dot(norm[j, rows], wq[layer, j], preferred_element_type=f32)
            return carry

        lax.fori_loop(0, CHUNKS, body, 0)

        def turn(v, g):
            n = v * lax.rsqrt(jnp.mean(v * v, axis=-1, keepdims=True) + epsilon) * g
            return n * cosf[rows, :] + pltpu.roll(n, HEAD // 2, 1) * sinf[rows, :]

        for i in range(4):
            turned = turn(mixed[rows, i * HEAD : (i + 1) * HEAD], qgain[layer])
            for h in range(start // PART, (start + count) // PART):
                for s in range(STEPS):
                    at = h * PART + s * SIDE - start
                    to = (s * 4 + i) * ROWS + h * SIDE
                    qs[to : to + SIDE, :] = turned[at : at + SIDE]
        nk[rows, :] = turn(mixed[rows, 4 * HEAD : 5 * HEAD], kgain[layer])
        nv[rows, :] = mixed[rows, 5 * HEAD : 6 * HEAD]

    row = lax.broadcasted_iota(jnp.int32, (128, 32), 0)
    col = lax.broadcasted_iota(jnp.int32, (128, 32), 1)
    fresh = jnp.logical_and(
        jnp.right_shift(row, 4) == jnp.bitwise_and(col, 7),
        jnp.right_shift(col, 3) <= jnp.bitwise_and(jnp.right_shift(row, 2), 3),
    )
    slot_index = lax.broadcasted_iota(jnp.int32, (16, SLOTS), 1).astype(f32)

    def attend(layer, h):
        if h == 0:
            for copy in kv[layer]:
                copy.wait()

        def body(b, carry):
            query = [qs[pl.ds(b * 8 + k, 16, stride=ROWS), :].astype(bf16) for k in range(8)]
            old = []
            for k in range(8):
                score = lax.dot_general(query[k], kbuf[b * 8 + k], NT, preferred_element_type=f32) * HEAD ** (-0.5)
                old.append(jnp.where(slot_index < limit[pl.ds(b * 8 + k, 1), :], score, -jnp.inf))
            old = jnp.concatenate(old, axis=0)
            part = [pl.ds(pl.multiple_of(h * (PART - SIDE) + s * SIDE + b * 8, 8), 8) for s in range(STEPS)]
            keys = jnp.concatenate([nk[w, :] for w in part], axis=0).astype(bf16)
            values = jnp.concatenate([nv[w, :] for w in part], axis=0).astype(bf16)
            new = lax.dot_general(jnp.concatenate(query, axis=0), keys, NT, preferred_element_type=f32) * HEAD ** (-0.5)
            new = jnp.where(fresh, new, -jnp.inf)
            top = jnp.maximum(jnp.max(old, axis=-1, keepdims=True), jnp.max(new, axis=-1, keepdims=True))
            old = jnp.exp(old - top)
            new = jnp.exp(new - top)
            below = jnp.sum(old, axis=-1, keepdims=True) + jnp.sum(new, axis=-1, keepdims=True)
            old = (old / below).astype(bf16)
            new = (new / below).astype(bf16)
            fresh_part = jnp.dot(new, values, preferred_element_type=f32)
            for k in range(8):
                rows = slice(k * 16, (k + 1) * 16)
                ao[pl.ds(b * 8 + k, 16, stride=ROWS), :] = (
                    jnp.dot(old[rows], vbuf[b * 8 + k], preferred_element_type=f32) + fresh_part[rows]
                )
            return carry

        lax.fori_loop(h * SIDE // 8, (h + 1) * SIDE // 8, body, 0)
        for s in range(STEPS):
            for i in range(4):
                start = (s * 4 + i) * ROWS + h * SIDE
                att[layer, h, t, s * SIDE : (s + 1) * SIDE, i * HEAD : (i + 1) * HEAD] = ao[
                    start : start + SIDE, :
                ].astype(bf16)

    def project_out(layer, h, before):
        total = jnp.zeros((PART, CHUNK), f32)
        for k in range(TP):
            total = total + lax.dot_general(
                att[layer, h, k], wo[layer, k // 4, :, (k % 4) * ATT : (k % 4 + 1) * ATT], NT,
                preferred_element_type=f32,
            )
        return (before.astype(f32) + total).astype(bf16)

    def att_ref(layer, h):
        return lambda k: att.at[layer, h, k]

    def hid_ref(h):
        return lambda k: hid.at[h, k]

    def out_ref(h):
        return lambda k: out.at[h, k]

    refs = [
        att_ref(0, 0), att_ref(0, 1), hid_ref(0), hid_ref(1), att_ref(1, 0), att_ref(1, 1), out_ref(0), out_ref(1)
    ]

    def first_out(h):
        hid[h, t] = project_out(0, h, resid[h * PART : (h + 1) * PART, :])
        g(1, 2 + h)

    def second_in(h):
        normalize(1, h * PART, PART, lambda rows, j: hid[h, j, rows, :])
        project_in(1, h * PART, PART)
        attend(1, h)
        g(1, 4 + h)

    keep = [pltpu.make_async_copy(hown.at[h], out.at[h, t], loc.at[3 * h]) for h in range(PARTS)]

    def second_out(h):
        hown[h] = project_out(1, h, hid[h, t])
        g(1, 6 + h, hown.at[h])
        keep[h].start()

    start_exchange()
    prepare()
    pack_o(0)
    pack_q(0)
    q(1,0)
    pack_o(1)
    for copy in load_x:
        copy.wait()
    normalize(0, 0, FLAT, lambda rows, j: xin[rows, j * CHUNK : (j + 1) * CHUNK])
    q(2,0)
    start_second()
    pick_own()
    q(3,0)
    pack_q(1)
    q(1,1)
    o(1,0)
    q(4,0)
    q(5,0)
    project_in(0,0,FLAT)
    attend(0,0)
    g(1,0)
    o(2,0)
    attend(0,1)
    g(1,1)
    load_kv(1)
    g(2,0)
    g(2,1)
    g(3,0)
    o(3,0)
    g(3,1)
    q(2,1)
    g(4,0)
    o(4,0)
    g(4,1)
    o(5,0)
    first_out(0)
    first_out(1)
    q(3,1)
    o(1,1)
    g(2,2)
    g(2,3)
    g(3,2)
    g(3,3)
    g(4,2)
    q(4,1)
    q(5,1)
    second_in(0)
    o(2,1)
    g(4,3)
    second_in(1)
    g(2,4)
    g(2,5)
    o(3,1)
    g(3,4)
    g(3,5)
    g(4,4)
    o(4,1)
    o(5,1)
    second_out(0)
    g(4,5)
    second_out(1)
    g(2,6)
    g(2,7)
    g(3,6)
    g(3,7)
    g(4,6)
    g(4,7)
    for copy in keep:
        copy.wait()
    for copy in sent:
        copy.wait_send()

    @pl.when(half_of_t != c)
    def _():
        sibling_slab().wait_send()


def fused(*operands):
    whole = pl.BlockSpec(memory_space=pltpu.VMEM)
    anywhere = pl.BlockSpec(memory_space=pl.ANY)
    dma = pltpu.SemaphoreType.DMA
    return pl.pallas_call(
        kernel,
        out_shape=jax.ShapeDtypeStruct((PARTS, TP, PART, CHUNK), bf16),
        in_specs=[anywhere] * 3 + [whole] * 5 + [anywhere] * 2,
        out_specs=anywhere,
        scratch_shapes=[
            pltpu.VMEM((LAYERS, CHUNKS, CHUNK, GROUP), bf16),
            pltpu.VMEM((LAYERS, 2, CHUNK, HALF), bf16),
            pltpu.VMEM((LAYERS, TP, PAD, GROUP), bf16),
            pltpu.VMEM((LAYERS, 2, PAD, HALF), bf16),
            pltpu.VMEM((TP * OWN, GROUP), f32),
            pltpu.VMEM((FLAT, D), bf16),
            pltpu.VMEM((CHUNKS, FLAT, CHUNK), bf16),
            pltpu.VMEM((PARTS, TP, PART, CHUNK), bf16),
            pltpu.VMEM((PARTS, PART, CHUNK), bf16),
            pltpu.VMEM((LAYERS, PARTS, TP, PART, ATT), bf16),
            pltpu.VMEM((ROWS, SLOTS, HEAD), bf16),
            pltpu.VMEM((ROWS, SLOTS, HEAD), bf16),
            pltpu.VMEM((16 * ROWS, HEAD), f32),
            pltpu.VMEM((16 * ROWS, HEAD), f32),
            pltpu.VMEM((FLAT, HEAD), f32),
            pltpu.VMEM((FLAT, HEAD), f32),
            pltpu.VMEM((FLAT, GROUP), f32),
            pltpu.VMEM((FLAT, CHUNK), f32),
            pltpu.VMEM((LAYERS * CHUNKS, CHUNK), f32),
            pltpu.VMEM((FLAT, HEAD), f32),
            pltpu.VMEM((FLAT, HEAD), f32),
            pltpu.VMEM((ROWS, SLOTS), f32),
            dma((LAYERS, TP)), dma((LAYERS, TP)),
            dma((LAYERS,)), dma((LAYERS, 3)),
            dma((LAYERS, 16)), dma((LAYERS, 16)),
            dma((LAYERS, 16)), dma((LAYERS, 16)),
            dma((4 * PARTS, 8)), dma((4 * PARTS, 8)),
            dma((4 + PARTS * STEPS,)),
        ],
        compiler_params=pltpu.CompilerParams(
            collective_id=0, has_side_effects=True, vmem_limit_bytes=60 * 1024 * 1024
        ),
    )(*operands)


def restore_kernel(hidden, natural):
    for p in range(CHUNKS):
        window = slice(p * 80 // 128 * 128, -(-(p + 1) * 80 // 128) * 128)
        wide = [hidden[0, k, :, window].astype(f32) for k in range(TP)]
        start = p * 80 % 128
        parts = [wide[k][:, start + core * OWN : start + (core + 1) * OWN] for core in range(2) for k in range(TP)]
        natural[0, :, p * CHUNK : (p + 1) * CHUNK] = jnp.concatenate(parts, axis=1).astype(bf16)


def restore(hidden):
    return pl.pallas_call(
        restore_kernel,
        out_shape=jax.ShapeDtypeStruct((STEPS, ROWS, D), bf16),
        grid=(PARTS, STEPS),
        in_specs=[pl.BlockSpec((1, TP, SIDE, CHUNK), lambda h, s: (h, 0, s, 0))],
        out_specs=pl.BlockSpec((1, SIDE, D), lambda h, s: (s, h, 0)),
        compiler_params=pltpu.CompilerParams(vmem_limit_bytes=32 * 1024 * 1024),
    )(hidden)


def on_device(
    inputs, qkv_weight, out_weight, norm_gain, query_gain, key_gain, stored_rotated_keys, stored_cache_values, lengths
):
    half = HEAD // 2
    frequency = rope_base ** (-jnp.arange(half, dtype=f32) / half)
    hidden = fused(
        inputs,
        qkv_weight.reshape(LAYERS * OWN, TP * GROUP),
        out_weight.reshape(LAYERS * OWN, TP * ATT),
        norm_gain,
        query_gain.reshape(LAYERS, 1, HEAD),
        key_gain.reshape(LAYERS, 1, HEAD),
        lengths.reshape(1, ROWS),
        jnp.concatenate([frequency, frequency]).reshape(1, HEAD),
        stored_rotated_keys.reshape(LAYERS, ROWS, SLOTS, HEAD),
        stored_cache_values.reshape(LAYERS, ROWS, SLOTS, HEAD),
    )
    return restore(hidden)


def solution(mesh):
    return jax.shard_map(
        on_device,
        mesh=mesh,
        in_specs=(
            P(None, "rep", None),
            P(None, ("rep", "tp"), None),
            P(None, ("rep", "tp"), None),
            P(),
            P(),
            P(),
            P(None, "rep", "tp", None, None),
            P(None, "rep", "tp", None, None),
            P("rep"),
        ),
        out_specs=P(None, "rep", None),
        check_vma=False,
    )
```
